32 devices in a mesh: groups: 2 (over y), pool: 4 (over z), tp: 2 (over x), sub: 2 (over core).
Axes of the slice: x: 2, y: 2, z: 4, core: 2. Of those that a mesh axis runs over, the one named last changes fastest.
Arguments:
- hidden: bfloat16 [128, 3, 8192], P('groups', None, 'pool'), parts along dimension 0, may hold values from -6 to 6
- query_weight: bfloat16 [8192, 8192], P('pool', ('tp', 'sub')), may hold values from -0.0625 to 0.0625
- key_weight: bfloat16 [8192, 1024], P('pool', ('tp', 'sub')), may hold values from -0.0625 to 0.0625
- value_weight: bfloat16 [8192, 1024], P('pool', ('tp', 'sub')), may hold values from -0.0625 to 0.0625
- key_cache_rows: bfloat16 [128, 8, 256, 128], P(('groups', 'pool'), ('tp', 'sub')), parts along dimension 0, may hold values from -6 to 6
- value_cache_rows: bfloat16 [128, 8, 256, 128], P(('groups', 'pool'), ('tp', 'sub')), parts along dimension 0, may hold values from -6 to 6
- adapter_down_weight: bfloat16 [16, 128, 8192], P(('groups', 'pool'), None, ('tp', 'sub')), parts along dimension 0, may hold values from -0.0625 to 0.0625
- adapter_up_query: bfloat16 [16, 64, 8192], P(('groups', 'pool'), None, ('tp', 'sub')), parts along dimension 0, may hold values from -0.75 to 0.75
- adapter_up_value: bfloat16 [16, 64, 1024], P(('groups', 'pool'), None, ('tp', 'sub')), parts along dimension 0, may hold values from -0.75 to 0.75
- request_adapter: int32 [128], P('groups'), parts along dimension 0, may hold values from 0 to 7, as said below
- row_request: int32 [128], P('groups'), parts along dimension 0, may hold values from 0 to 63, as said below
- lengths: int32 [128], P('groups'), parts along dimension 0, may hold values from 1 to 256, as said below
Outputs:
- attended: bfloat16 [128, 3, 8192], P(('groups', 'pool'), None, ('tp', 'sub')), parts along dimension 0
The draws below stay inside these ranges and needn't reach their ends.
There are 2 independent parts, one for each index of `groups`. The reference program is written for one: setup_inputs(seed, part) draws one part's arguments, and reference() takes and returns one part's arrays. A program takes and returns all parts, laid end to end along the dimension named above; an argument that names none is the same for every part. Nothing has to cross between parts.
Inputs may be any that keep to these rules, and one draw needn't show every extreme that they name: `request_adapter`: with owner = adapter // 2: among the rows of one device (batch rows b with equal b // 16, row b holding request row_request[b]) at most 8 use adapters of one owner, and in every draw some owner is used by exactly 8 rows of every device. `row_request`: A permutation: each request sits in exactly one batch row. `lengths`: some request holds all 256 positions.
All inputs are finite; a program needn't handle non-finite values.
Results may differ from the reference program's by a relative error of at most 0.03.
Values may be sent and summed in bfloat16 or wider, within the bound.
No kernel may reach another device: no remote copies, remote signals or barrier semaphores. Data moves between devices by JAX's collectives and lax.ppermute only.
A program may use at most 128 MiB of HBM per device.

```python
import math
import jax
import jax.numpy as jnp
from jax import lax

MODEL_WIDTH = 8192
QUERY_HEADS = 64
KEY_VALUE_HEADS = 8
HEAD_SIZE = 128
ADAPTER_RANK = 64
STEPS = 3
CACHE = 256
REQ_DEV = 16
ADP_DEV = 2
REQUESTS = 64
ADAPTER_TOTAL = 8
CAP = 8
N_POOL = 4


def assignment(key):
    key = jax.random.fold_in(key, 11)
    owners = ADAPTER_TOTAL // ADP_DEV
    slots = owners * CAP
    blocks = REQUESTS // REQ_DEV
    hot_owner = jax.random.randint(jax.random.fold_in(key, 1), (), 0, owners)
    slot_owner = jnp.arange(slots, dtype=jnp.int32) // CAP

    def block_owners(block_key):
        first_key, second_key = jax.random.split(block_key)
        scores = jax.random.permutation(first_key, slots).astype(jnp.int32)
        scores = jnp.where(slot_owner == hot_owner, -1 - jnp.arange(slots, dtype=jnp.int32), scores)
        chosen = slot_owner[jnp.argsort(scores, stable=True)[:REQ_DEV]]
        return jax.random.permutation(second_key, chosen)
    block_keys = jax.random.split(jax.random.fold_in(key, 2), blocks)
    row_owner = jax.vmap(block_owners)(block_keys).reshape(-1)
    within = jax.random.randint(jax.random.fold_in(key, 3), (REQUESTS,), 0, ADP_DEV)
    row_adapter = row_owner * ADP_DEV + within
    order = jax.random.permutation(jax.random.fold_in(key, 4), REQUESTS).astype(jnp.int32)
    inverse = jnp.argsort(order, stable=True)
    return (row_adapter[inverse].astype(jnp.int32), order)


def draw_request_adapter(key, part):
    return assignment(key)[0]


def draw_row_request(key, part):
    return assignment(key)[1]


def draw_lengths(key, part):
    key = jax.random.fold_in(key, 7)
    first_key, second_key = jax.random.split(key)
    spread = jax.random.randint(first_key, (REQUESTS,), 1, CACHE + 1)
    longest = jax.random.randint(second_key, (), 0, REQUESTS)
    return jnp.where(jnp.arange(REQUESTS) == longest, CACHE, spread).astype(jnp.int32)


def spiked(result, stream_key, source, target, blocks, factor):
    owner, partner = [(jnp.arange(result.shape[position]) // (result.shape[position] // blocks)).reshape([-1 if axis == position else 1 for axis in range(result.ndim)]) for position in (source, target)]
    chosen = jax.random.permutation(stream_key, blocks)[partner]
    strong = (owner == chosen) | (owner == (partner + blocks // 2) % blocks)
    return jnp.where(strong, factor * result, result)


def steps_of(rng, extent, cuts, least, high):
    loudness, own = 1.0, jax.random.fold_in(rng, 6)
    for dim, shards_of in cuts:
        draws = jnp.exp(jax.random.uniform(jax.random.fold_in(own, dim), (shards_of,), jnp.float32, least / len(cuts), high / len(cuts)))
        loudness = loudness * jnp.repeat(draws, extent[dim] // shards_of).reshape([-1 if axis == dim else 1 for axis in range(len(extent))])
    return loudness


def gaussian(own_key, dims, deviation, bound, cuts=(), kind=jnp.bfloat16):
    array = jax.random.normal(own_key, dims, jnp.float32) * deviation
    if len(cuts) > 0:
        array = steps_of(own_key, dims, cuts, -0.22, 0.18) * array
    return jnp.clip(array, min=-bound, max=bound).astype(kind)


def noise_with(stream_key, extent, scale, bound, pieces, heavy, kind=jnp.bfloat16):
    entries = scale * jax.random.normal(stream_key, extent, jnp.float32)
    if pieces:
        entries = entries * steps_of(stream_key, extent, pieces, -0.22, 0.18)
    return jnp.clip(spiked(entries, jax.random.fold_in(stream_key, 3), *heavy), -bound, bound).astype(kind)


def setup_inputs(seed: int = 0, part: int = 0) -> dict:
    splits = jax.random.split(jax.random.key(seed), 13)
    part_keys = jax.random.split(jax.random.fold_in(splits[12], part), 13)
    hidden = noise_with(part_keys[0], (REQUESTS, STEPS, MODEL_WIDTH), 1.0, 6.0, ((2, 4),), (2, 0, 4, 2.0))
    query_weight = gaussian(splits[1], (MODEL_WIDTH, QUERY_HEADS * HEAD_SIZE), MODEL_WIDTH ** -0.5, 0.0625, ((0, 4), (1, 4)))
    key_weight = gaussian(splits[2], (MODEL_WIDTH, KEY_VALUE_HEADS * HEAD_SIZE), MODEL_WIDTH ** -0.5, 0.0625, ((0, 4), (1, 4)))
    value_weight = gaussian(splits[3], (MODEL_WIDTH, KEY_VALUE_HEADS * HEAD_SIZE), MODEL_WIDTH ** -0.5, 0.0625, ((0, 4), (1, 4)))
    key_cache_rows = gaussian(part_keys[4], (REQUESTS, KEY_VALUE_HEADS, CACHE, HEAD_SIZE), 1.0, 6.0, ((0, 4), (1, 4)))
    value_cache_rows = gaussian(part_keys[5], (REQUESTS, KEY_VALUE_HEADS, CACHE, HEAD_SIZE), 1.0, 6.0, ((0, 4), (1, 4)))
    adapter_down_weight = gaussian(part_keys[6], (ADAPTER_TOTAL, 2 * ADAPTER_RANK, MODEL_WIDTH), MODEL_WIDTH ** -0.5, 0.0625, ((0, 4), (2, 4)))
    adapter_up_query = gaussian(part_keys[7], (ADAPTER_TOTAL, ADAPTER_RANK, QUERY_HEADS * HEAD_SIZE), ADAPTER_RANK ** -0.5, 0.75, ((0, 4), (2, 4)))
    adapter_up_value = gaussian(part_keys[8], (ADAPTER_TOTAL, ADAPTER_RANK, KEY_VALUE_HEADS * HEAD_SIZE), ADAPTER_RANK ** -0.5, 0.75, ((0, 4), (2, 4)))
    request_adapter = draw_request_adapter(jax.random.fold_in(jax.random.fold_in(splits[12], part), 71), part)
    row_request = draw_row_request(jax.random.fold_in(jax.random.fold_in(splits[12], part), 71), part)
    lengths = draw_lengths(jax.random.fold_in(jax.random.fold_in(splits[12], part), 71), part)
    return dict(hidden=hidden, query_weight=query_weight, key_weight=key_weight, value_weight=value_weight, key_cache_rows=key_cache_rows, value_cache_rows=value_cache_rows, adapter_down_weight=adapter_down_weight, adapter_up_query=adapter_up_query, adapter_up_value=adapter_up_value, request_adapter=request_adapter, row_request=row_request, lengths=lengths)


ROPE_BASE = 500000.0

def rotate(values, positions):
    head_dim = values.shape[-1]
    half_dim = head_dim // 2
    inverse_freq = ROPE_BASE ** (-2.0 * jnp.arange(half_dim, dtype=jnp.float32) / head_dim)
    angles = positions.astype(jnp.float32)[:, :, None, None] * inverse_freq
    cosine = jnp.cos(angles)
    sine_part = jnp.sin(angles)
    first = values[..., :half_dim]
    second = values[..., half_dim:]
    return jnp.concatenate([first * cosine - second * sine_part, second * cosine + first * sine_part], -1)

def attend(queries, keys_new, values_new, key_cache_rows, value_cache_rows, row_length):
    rows, steps, heads, head_dim = queries.shape
    kv_heads = key_cache_rows.shape[1]
    group_size = heads // kv_heads
    grouped = queries.reshape(rows, steps, kv_heads, group_size, head_dim).transpose(0, 2, 1, 3, 4)
    grouped = grouped.reshape(rows, kv_heads, steps * group_size, head_dim).astype(jnp.float32)
    scale_factor = 1.0 / math.sqrt(head_dim)
    scores_cache = jnp.einsum('rkqh,rkth->rkqt', grouped, key_cache_rows.astype(jnp.float32)) * scale_factor
    new_keys = keys_new.transpose(0, 2, 1, 3).astype(jnp.float32)
    new_values = values_new.transpose(0, 2, 1, 3).astype(jnp.float32)
    scores_new = jnp.einsum('rkqh,rksh->rkqs', grouped, new_keys) * scale_factor
    live_cache = jnp.arange(key_cache_rows.shape[2], dtype=jnp.int32)[None, :] < row_length[:, None]
    query_step = jnp.arange(steps * group_size, dtype=jnp.int32) // group_size
    live_new = jnp.arange(steps, dtype=jnp.int32)[None, :] <= query_step[:, None]
    weights_cache = jnp.where(live_cache[:, None, None, :], jnp.exp(scores_cache), 0.0)
    weights_new = jnp.where(live_new[None, None], jnp.exp(scores_new), 0.0)
    denominator = lax.optimization_barrier(jnp.sum(weights_cache, -1)) + lax.optimization_barrier(jnp.sum(weights_new, -1))
    probs_cache = (weights_cache / denominator[..., None]).astype(jnp.bfloat16)
    probs_new = (weights_new / denominator[..., None]).astype(jnp.bfloat16)
    mixed = jnp.einsum('rkqt,rkth->rkqh', probs_cache.astype(jnp.float32), value_cache_rows.astype(jnp.float32))
    mixed = mixed + jnp.einsum('rkqs,rksh->rkqh', probs_new.astype(jnp.float32), new_values)
    mixed = mixed.reshape(rows, kv_heads, steps, group_size, head_dim).transpose(0, 2, 1, 3, 4)
    return mixed.reshape(rows, steps, heads * head_dim).astype(jnp.bfloat16)

def reference(hidden, query_weight, key_weight, value_weight, key_cache_rows, value_cache_rows, adapter_down_weight, adapter_up_query, adapter_up_value, request_adapter, row_request, lengths):
    row_adapter = request_adapter[row_request]
    row_length = lengths[row_request]
    w_all = jnp.concatenate([query_weight, key_weight, value_weight], 1)
    q_cols = QUERY_HEADS * HEAD_SIZE
    kv_cols = KEY_VALUE_HEADS * HEAD_SIZE
    portion_width = MODEL_WIDTH // N_POOL
    flat_rows = hidden.reshape(REQUESTS * STEPS, MODEL_WIDTH)

    def add_shard(running, shard_index):
        piece = lax.dynamic_slice_in_dim(flat_rows, shard_index * portion_width, portion_width, 1)
        block = lax.dynamic_slice_in_dim(w_all, shard_index * portion_width, portion_width, 0)
        shard_term = jnp.dot(piece, block, preferred_element_type=jnp.float32).astype(jnp.bfloat16)
        shard_term = lax.optimization_barrier(shard_term)
        return (running + shard_term.astype(jnp.float32), None)
    projected, _ = lax.scan(add_shard, jnp.zeros((REQUESTS * STEPS, w_all.shape[1]), jnp.float32), jnp.arange(N_POOL, dtype=jnp.int32))
    flat_adapter = jnp.repeat(row_adapter, STEPS)

    def add_adapter(carry, adapter_position):
        delta_q, delta_v = carry
        down_weight_block = lax.dynamic_index_in_dim(adapter_down_weight, adapter_position, 0, keepdims=False)
        query_up_weight = lax.dynamic_index_in_dim(adapter_up_query, adapter_position, 0, keepdims=False)
        value_up_weight = lax.dynamic_index_in_dim(adapter_up_value, adapter_position, 0, keepdims=False)
        shrunk = jnp.dot(flat_rows, down_weight_block.T, preferred_element_type=jnp.float32)
        low_rank = shrunk.astype(jnp.bfloat16)
        term_q = jnp.dot(low_rank[:, :ADAPTER_RANK], query_up_weight, preferred_element_type=jnp.float32)
        term_v = jnp.dot(low_rank[:, ADAPTER_RANK:], value_up_weight, preferred_element_type=jnp.float32)
        chosen_rows = (flat_adapter == adapter_position)[:, None]
        return ((delta_q + jnp.where(chosen_rows, term_q, 0.0), delta_v + jnp.where(chosen_rows, term_v, 0.0)), None)
    zeros_q = jnp.zeros((REQUESTS * STEPS, q_cols), jnp.float32)
    zeros_v = jnp.zeros((REQUESTS * STEPS, kv_cols), jnp.float32)
    (delta_q, delta_v), _ = lax.scan(add_adapter, (zeros_q, zeros_v), jnp.arange(ADAPTER_TOTAL, dtype=jnp.int32))
    delta_q = lax.optimization_barrier(delta_q.astype(jnp.bfloat16)).astype(jnp.float32)
    delta_v = lax.optimization_barrier(delta_v.astype(jnp.bfloat16)).astype(jnp.float32)
    positions = row_length[:, None] + jnp.arange(STEPS, dtype=jnp.int32)[None, :]
    raw_q = (projected[:, :q_cols] + delta_q).reshape(REQUESTS, STEPS, QUERY_HEADS, HEAD_SIZE)
    raw_k = projected[:, q_cols:q_cols + kv_cols].reshape(REQUESTS, STEPS, KEY_VALUE_HEADS, HEAD_SIZE)
    raw_v = (projected[:, q_cols + kv_cols:] + delta_v).reshape(REQUESTS, STEPS, KEY_VALUE_HEADS, HEAD_SIZE)
    queries = rotate(raw_q, positions).astype(jnp.bfloat16)
    keys_new = rotate(raw_k, positions).astype(jnp.bfloat16)
    values_new = raw_v.astype(jnp.bfloat16)
    return attend(queries, keys_new, values_new, key_cache_rows, value_cache_rows, row_length)
```

```python
import functools
import math

import jax
import jax.numpy as jnp
from jax import lax
from jax.experimental import pallas as pl
from jax.experimental.pallas import tpu as pltpu
from jax.sharding import PartitionSpec as P

ROPE_BASE = 500000.0
BF16 = jnp.bfloat16
F32 = jnp.float32
FEATURE_AXES = ("tp", "sub")
CARRIER = ((0, 3, 2, 1), (2, 1, 0, 3), (3, 1, 2, 0), (1, 2, 0, 3))
VMEM_LIMIT = 48 * 1024 * 1024


def call(body, out_shape, args, in_specs=None, out_specs=None, grid=None, scratch=(), flops=0, bytes_=0, **more):
    whole = pl.BlockSpec(memory_space=pltpu.VMEM)
    kwargs = {} if grid is None else {"grid": grid}
    if in_specs is None:
        in_specs = [whole] * len(args)
    if out_specs is None:
        out_specs = jax.tree.map(lambda _: whole, out_shape)
    return pl.pallas_call(
        body,
        out_shape=out_shape,
        in_specs=in_specs,
        out_specs=out_specs,
        scratch_shapes=list(scratch),
        compiler_params=pltpu.CompilerParams(vmem_limit_bytes=VMEM_LIMIT),
        cost_estimate=pl.CostEstimate(flops=flops, bytes_accessed=bytes_, transcendentals=0),
        **kwargs,
        **more,
    )(*args)


VMEM = pl.BlockSpec(memory_space=pltpu.VMEM)
SMEM = pl.BlockSpec(memory_space=pltpu.SMEM)


def iota(shape, dim):
    return lax.broadcasted_iota(jnp.int32, shape, dim)


def nn(a, b):
    return lax.dot_general(a, b, (((1,), (0,)), ((), ())), preferred_element_type=F32)


def nt(a, b):
    return lax.dot_general(a, b, (((1,), (1,)), ((), ())), preferred_element_type=F32)


def tn(a, b):
    return lax.dot_general(a, b, (((0,), (0,)), ((), ())), preferred_element_type=F32)


def row_facts(row_request, request_values, home_rows, resident):
    rows = row_request.shape[1]
    across, down = iota((rows, rows), 1), iota((rows, rows), 0)
    eye = across == down
    request_col = jnp.sum(jnp.where(eye, row_request.astype(F32), 0.0), 1, keepdims=True)
    held = request_col == across.astype(F32)
    adapter_col = jnp.sum(jnp.where(held, request_values.astype(F32), 0.0), 1, keepdims=True)
    adapter_row = jnp.sum(jnp.where(eye, adapter_col, 0.0), 0, keepdims=True)
    owner_col = jnp.floor((adapter_col + 0.5) / resident)
    owner_row = jnp.floor((adapter_row + 0.5) / resident)
    before = (owner_col == owner_row) & (down < across) & (down // home_rows == across // home_rows)
    slot_row = jnp.sum(jnp.where(before, 1.0, 0.0), 0, keepdims=True)
    return adapter_row, owner_row, slot_row


def slot_table(owner_row, slot_row, owner, home_rows, cap):
    rows = owner_row.shape[1]
    places = rows // home_rows * cap
    place, row = iota((places, rows), 0), iota((places, rows), 1)
    return (
        (owner_row == owner.astype(F32))
        & (place // cap == row // home_rows)
        & (slot_row == (place % cap).astype(F32))
    )


def select_body(home_rows, cap, resident, owners_here, rr_ref, ra_ref, where_ref, hid_ref, *outs):
    _, owner_row, slot_row = row_facts(rr_ref[...], ra_ref[...], home_rows, resident)
    for i, out in enumerate(outs):
        table = slot_table(owner_row, slot_row, where_ref[1 + i], home_rows, cap).astype(BF16)
        places = table.shape[0]
        for s in range(hid_ref.shape[0]):
            out[s * places : (s + 1) * places] = nn(table, hid_ref[s]).astype(BF16)


def project_body(home_rows, homes, emit_chunks, where_ref, x_ref, q_ref, k_ref, v_ref, *rest):
    steps, rows = x_ref.shape[0] // (homes * home_rows), homes * home_rows
    tile = q_ref.shape[1]
    head_dim = k_ref.shape[1]
    if emit_chunks:
        outs, scr, scr_kv = rest[:homes], rest[homes], rest[homes + 1]
    else:
        (out,) = rest
    i = pl.program_id(0)
    columns = pl.ds(pl.multiple_of(i * tile, tile), tile)
    product = nn(x_ref[...], q_ref[...])
    q_cols = pl.num_programs(0) * tile

    def put(value, source, where):
        source[...] = value
        for d in range(homes):
            home = where_ref[0] ^ d
            for s in range(steps):
                begin = pl.multiple_of(s * rows + home * home_rows, home_rows)
                outs[d][s * home_rows : (s + 1) * home_rows, where] = source[
                    pl.ds(begin, home_rows), :
                ].astype(BF16)

    if emit_chunks:
        put(product, scr, columns)
    else:
        out[:, columns] = product

    @pl.when(i == 0)
    def _():
        kv = jnp.concatenate([nn(x_ref[...], k_ref[...]), nn(x_ref[...], v_ref[...])], 1)
        width = outs[0].shape[1] if emit_chunks else out.shape[1]
        if emit_chunks:
            put(kv, scr_kv, slice(width - 2 * head_dim, width))
        else:
            out[:, width - 2 * head_dim :] = kv


def shrink_body(home_rows, cap, resident, parts, rr_ref, ra_ref, where_ref, down_ref, *rest):
    sent, out = rest[:-1], rest[-1]
    adapter_row, owner_row, slot_row = row_facts(rr_ref[...], ra_ref[...], home_rows, resident)
    me = where_ref[0]
    table = slot_table(owner_row, slot_row, me, home_rows, cap)
    local = jnp.sum(jnp.where(table, adapter_row - (me * resident).astype(F32) + 1.0, 0.0), 1, keepdims=True) - 1.0
    places = table.shape[0]
    steps = sent[0].shape[0] // places
    local = jnp.concatenate([local] * steps, 0)
    width = sent[0].shape[1]
    total = None
    for a in range(resident):
        term = None
        for i in range(parts):
            if parts == 1:
                block = down_ref[a]
            else:
                part = lax.rem(me + parts * places - i, parts)
                block = down_ref[a, :, pl.ds(pl.multiple_of(part * width, width), width)]
            piece = nt(sent[i][...], block)
            term = piece if term is None else term + piece
        term = jnp.where(local == float(a), term, 0.0)
        total = term if total is None else total + term
    out[...] = total.astype(BF16)


def expand_body(home_rows, homes, cap, resident, early, late, rr_ref, ra_ref, where_ref, upq_ref, upv_ref, *rest):
    n_parts = len(rest) - len(late) - homes * (len(early) + len(late)) - (1 if late else 0)
    shares, rest = rest[:n_parts], rest[n_parts:]
    partials, rest = rest[: len(late)], rest[len(late) :]
    early_outs, rest = rest[: homes * len(early)], rest[homes * len(early) :]
    late_outs, rest = rest[: homes * len(late)], rest[homes * len(late) :]
    adapter_row, owner_row, slot_row = row_facts(rr_ref[...], ra_ref[...], home_rows, resident)
    me = where_ref[0]
    table = slot_table(owner_row, slot_row, me, home_rows, cap)
    places, rows = table.shape
    local = jnp.sum(jnp.where(table, adapter_row - (me * resident).astype(F32) + 1.0, 0.0), 1, keepdims=True) - 1.0
    spread = table.astype(BF16)
    shrunk = shares[0][...].astype(F32)
    for share in shares[1:]:
        shrunk = shrunk + share[...].astype(F32)
    steps = shrunk.shape[0] // places
    local = jnp.concatenate([local] * steps, 0)
    rank = upq_ref.shape[1]
    low_q, low_v = shrunk[:, :rank], shrunk[:, rank:]
    masked_q = [jnp.where(local == float(a), low_q, 0.0).astype(BF16) for a in range(resident)]
    masked_v = [jnp.where(local == float(a), low_v, 0.0).astype(BF16) for a in range(resident)]
    kv_heads = len(early) + len(late)
    width_q = upq_ref.shape[2] // kv_heads
    width_v = upv_ref.shape[2] // kv_heads

    def up(h):
        delta_q = delta_v = None
        for a in range(resident):
            term_q = nn(masked_q[a], upq_ref[a, :, h * width_q : (h + 1) * width_q])
            term_v = nn(masked_v[a], upv_ref[a, :, h * width_v : (h + 1) * width_v])
            delta_q = term_q if delta_q is None else delta_q + term_q
            delta_v = term_v if delta_v is None else delta_v + term_v
        return delta_q, delta_v

    for n, h in enumerate(early):
        both = jnp.concatenate(up(h), 1)
        scr = rest[-1]
        scr[: both.shape[0], : both.shape[1]] = both
        for d in range(homes):
            home = me ^ d
            pieces = []
            for s in range(steps):
                begin = pl.multiple_of(s * places + home * cap, cap)
                pieces.append(scr[pl.ds(begin, cap), : both.shape[1]])
            early_outs[n * homes + d][...] = jnp.concatenate(pieces, 0).astype(BF16)
    for n, h in enumerate(late):
        delta_q, delta_v = up(h)
        scr = rest[-1]
        for s in range(steps):
            here = slice(s * places, (s + 1) * places)
            there = slice(s * rows, (s + 1) * rows)
            scr[there, :width_q] = partials[n][there, :width_q] + tn(spread, delta_q[here].astype(BF16))
            scr[there, width_q : width_q + width_v] = partials[n][there, width_q : width_q + width_v]
            scr[there, width_q + width_v :] = partials[n][there, width_q + width_v :] + tn(
                spread, delta_v[here].astype(BF16)
            )
        for d in range(homes):
            home = me ^ d
            for s in range(steps):
                begin = pl.multiple_of(s * rows + home * home_rows, home_rows)
                late_outs[n * homes + d][s * home_rows : (s + 1) * home_rows, :] = scr[
                    pl.ds(begin, home_rows), :
                ].astype(BF16)


def facts_body(home_rows, homes, cap, resident, head_dim, steps, rr_ref, ra_ref, len_ref, where_ref, cos_ref, sin_ref, *places_out):
    _, owner_row, slot_row = row_facts(rr_ref[...], ra_ref[...], home_rows, resident)
    length_row, _, _ = row_facts(rr_ref[...], len_ref[...], home_rows, resident)
    me = where_ref[0]
    local_rows = steps * home_rows
    rows = rr_ref.shape[1]
    row, batch = iota((local_rows, rows), 0), iota((local_rows, rows), 1)
    mine = batch == me * home_rows + row % home_rows
    length = jnp.sum(jnp.where(mine, length_row, 0.0), 1, keepdims=True)
    owner = jnp.sum(jnp.where(mine, owner_row, 0.0), 1, keepdims=True)
    slot = jnp.sum(jnp.where(mine, slot_row, 0.0), 1, keepdims=True)
    lane = iota((local_rows, head_dim), 1)
    step = iota((local_rows, head_dim), 0) // home_rows
    half = head_dim // 2
    entry = (lane % half).astype(F32)
    inverse_freq = jnp.exp(entry * (-2.0 * math.log(ROPE_BASE) / head_dim))
    angle = (length + step.astype(F32)) * inverse_freq
    cos_ref[...] = jnp.cos(angle)
    sin_ref[...] = jnp.where(lane < half, -1.0, 1.0) * jnp.sin(angle)
    for d, out in enumerate(places_out):
        place = iota((local_rows, steps * cap), 1)
        local = iota((local_rows, steps * cap), 0)
        out[...] = (
            (owner == (me ^ d).astype(F32))
            & (place // cap == local // home_rows)
            & (slot == (place % cap).astype(F32))
        ).astype(BF16)


def attend_body(home_rows, homes, steps, cache_head, early, where_ref, rr_ref, len_ref, cos_ref, sin_ref, kc_ref, vc_ref, *rest):
    chunks, rest = rest[:homes], rest[homes:]
    if early:
        places, rest = rest[:homes], rest[homes:]
        deltas, rest = rest[:homes], rest[homes:]
    out, q_scr, o_scr, d_scr = rest[-4:]
    local_rows = steps * home_rows
    head_dim = kc_ref.shape[3]
    cached = kc_ref.shape[2]
    heads = (chunks[0].shape[1] - 2 * head_dim) // head_dim
    width_q = heads * head_dim
    scale = 1.0 / math.sqrt(head_dim)
    cos, sin = cos_ref[...], sin_ref[...]

    def rope(v):
        return v * cos + pltpu.roll(v, head_dim // 2, 1) * sin

    def projected(begin, delta_begin):
        total = None
        for chunk in chunks:
            piece = chunk[:, begin : begin + head_dim].astype(F32)
            total = piece if total is None else total + piece
        if early and delta_begin is not None:
            delta = None
            for place, piece in zip(places, deltas):
                term = nn(place[...], piece[:, delta_begin : delta_begin + head_dim])
                delta = term if delta is None else delta + term
            total = total + delta
        return total

    key_new = rope(projected(width_q, None)).astype(BF16)
    value_new = projected(width_q + head_dim, width_q).astype(BF16)
    row, col = iota((local_rows, local_rows), 0), iota((local_rows, local_rows), 1)
    live = (row % home_rows == col % home_rows) & (col // home_rows <= row // home_rows)
    new_weights = []
    for n in range(heads):
        query = rope(projected(n * head_dim, n * head_dim)).astype(BF16)
        here = slice(n * local_rows, (n + 1) * local_rows)
        q_scr[here, :] = query.astype(F32)
        weight = jnp.where(live, jnp.exp(nt(query, key_new) * scale), 0.0)
        new_weights.append(weight)
        d_scr[here, :] = jnp.broadcast_to(jnp.sum(weight, 1, keepdims=True), (local_rows, head_dim))
    queries_row = heads * steps
    spot = iota((queries_row, cached), 1)
    for b in range(home_rows):
        length = len_ref[0, rr_ref[0, where_ref[0] * home_rows + b]]
        strided = pl.ds(b, queries_row, stride=home_rows)
        query = q_scr[strided, :].astype(BF16)
        weight = jnp.where(spot < length, jnp.exp(nt(query, kc_ref[b, 0]) * scale), 0.0)
        total = jnp.sum(weight, 1, keepdims=True) + d_scr[strided, :][:, :1]
        d_scr[strided, :] = jnp.broadcast_to(total, (queries_row, head_dim))
        o_scr[strided, :] = nn((weight / total).astype(BF16), vc_ref[b, 0])
    for n in range(heads):
        here = slice(n * local_rows, (n + 1) * local_rows)
        probs = (new_weights[n] / d_scr[here, :local_rows]).astype(BF16)
        out[:, n * head_dim : (n + 1) * head_dim] = (o_scr[here, :] + nn(probs, value_new)).astype(BF16)


def on_device(
    hidden,
    query_weight,
    key_weight,
    value_weight,
    key_cache_rows,
    value_cache_rows,
    adapter_down_weight,
    adapter_up_query,
    adapter_up_value,
    request_adapter,
    row_request,
    lengths,
):
    homes = lax.axis_size("pool")
    features = lax.axis_size(FEATURE_AXES)
    home_rows, kv_here, cached, head_dim = key_cache_rows.shape
    rows, steps, slice_width = hidden.shape
    resident = adapter_down_weight.shape[0]
    rank = adapter_up_query.shape[1]
    q_cols = query_weight.shape[1] // kv_here
    cap = max(2, 2 * home_rows // homes)
    places = homes * cap
    fold = homes // features
    local_rows = steps * home_rows
    width = q_cols + 2 * head_dim
    shape = jax.ShapeDtypeStruct

    pool_here = lax.axis_index("pool")
    feature_here = lax.axis_index(FEATURE_AXES)
    tuned = homes == len(CARRIER) and features == len(CARRIER)
    if tuned:
        targets = [[CARRIER[q].index(g) for g in range(features)] for q in range(homes)]
        target = sum(
            jnp.where((pool_here == q) & (feature_here == g), targets[q][g], 0)
            for q in range(homes)
            for g in range(features)
        )
        owners = [target]
        perms = [[(q * features + g, targets[q][g] * features + q) for q in range(homes) for g in range(features)]]
    else:
        owners = [feature_here * fold + (i + pool_here) % fold for i in range(fold)]
        perms = [
            [
                (q * features + g, (g * fold + (i + q) % fold) * features + q // fold)
                for q in range(homes)
                for g in range(features)
            ]
            for i in range(fold)
        ]
    where = jnp.stack([pool_here, *owners]).astype(jnp.int32)
    rr, ra, ln = row_request.reshape(1, rows), request_adapter.reshape(1, rows), lengths.reshape(1, rows)
    by_step = hidden.transpose(1, 0, 2)
    x = by_step.reshape(steps * rows, slice_width)
    early = tuple(range(kv_here // 2))
    late = tuple(range(kv_here // 2, kv_here))

    selected = call(
        functools.partial(select_body, home_rows, cap, resident, len(owners)),
        [shape((steps * places, slice_width), BF16)] * fold,
        (rr, ra, where, by_step),
        in_specs=[VMEM, VMEM, SMEM, VMEM],
        flops=2 * steps * places * rows * slice_width,
        bytes_=2 * steps * (rows + places) * slice_width,
    )
    sent = [lax.ppermute(s, ("pool", *FEATURE_AXES), perm) for s, perm in zip(selected, perms)]

    tile = min(256, q_cols)
    tiles = q_cols // tile

    def project(h, emit_chunks):
        out_shape = (
            [shape((local_rows, width), BF16)] * homes if emit_chunks else [shape((steps * rows, width), F32)]
        )
        return call(
            functools.partial(project_body, home_rows, homes, emit_chunks),
            out_shape,
            (where, x, query_weight, key_weight, value_weight),
            in_specs=[
                SMEM,
                pl.BlockSpec((steps * rows, slice_width), lambda i: (0, 0)),
                pl.BlockSpec((slice_width, tile), lambda i: (0, h * tiles + i)),
                pl.BlockSpec((slice_width, head_dim), lambda i: (0, h)),
                pl.BlockSpec((slice_width, head_dim), lambda i: (0, h)),
            ],
            out_specs=[pl.BlockSpec(s.shape, lambda i: (0, 0)) for s in out_shape],
            grid=(tiles,),
            scratch=[pltpu.VMEM((steps * rows, tile), F32), pltpu.VMEM((steps * rows, 2 * head_dim), F32)]
            if emit_chunks
            else [],
            flops=2 * steps * rows * slice_width * width,
            bytes_=2 * slice_width * width,
        )

    def to_home(pieces):
        return [pieces[0]] + [
            lax.ppermute(pieces[d], "pool", [(i, i ^ d) for i in range(homes)]) for d in range(1, homes)
        ]

    chunks = {}
    for h in early:
        chunks[h] = to_home(project(h, True))
    partials = [project(h, False)[0] for h in late]
    facts = call(
        functools.partial(facts_body, home_rows, homes, cap, resident, head_dim, steps),
        [shape((local_rows, head_dim), F32)] * 2 + [shape((local_rows, steps * cap), BF16)] * homes,
        (rr, ra, ln, where),
        in_specs=[VMEM, VMEM, VMEM, SMEM],
        flops=10**7,
        bytes_=10**5,
    )
    cos, sin, spots = facts[0], facts[1], facts[2:]

    share = call(
        functools.partial(shrink_body, home_rows, cap, resident, fold),
        shape((steps * places, 2 * rank), BF16),
        (rr, ra, where, adapter_down_weight, *sent),
        in_specs=[VMEM, VMEM, SMEM] + [VMEM] * (1 + fold),
        flops=4 * steps * places * rank * slice_width * fold * resident,
        bytes_=4 * resident * rank * slice_width * fold,
    )
    shares = [share] + [
        lax.ppermute(share, FEATURE_AXES, [(i, i ^ d) for i in range(features)]) for d in range(1, features)
    ]
    grown = call(
        functools.partial(expand_body, home_rows, homes, cap, resident, early, late),
        [shape((steps * cap, q_cols + head_dim), BF16)] * (homes * len(early))
        + [shape((local_rows, width), BF16)] * (homes * len(late)),
        (rr, ra, where, adapter_up_query, adapter_up_value, *shares, *partials),
        in_specs=[VMEM, VMEM, SMEM] + [VMEM] * (2 + len(shares) + len(partials)),
        scratch=[pltpu.VMEM((max(rows, places) * steps, width), F32)],
        flops=2 * steps * places * rank * resident * q_cols * kv_here,
        bytes_=2 * resident * rank * q_cols * kv_here,
    )
    deltas = {}
    for n, h in enumerate(early):
        deltas[h] = to_home(grown[n * homes : (n + 1) * homes])
    grown = grown[homes * len(early) :]
    for n, h in enumerate(late):
        chunks[h] = to_home(grown[n * homes : (n + 1) * homes])

    out = None
    for h in range(kv_here):
        is_early = h in early
        extra = (*spots, *deltas[h]) if is_early else ()
        args = (where, rr, ln, cos, sin, key_cache_rows, value_cache_rows, *chunks[h], *extra)
        cache_spec = pl.BlockSpec((home_rows, 1, cached, head_dim), lambda i: (0, h, 0, 0))
        in_specs = [SMEM, SMEM, SMEM, VMEM, VMEM, cache_spec, cache_spec] + [VMEM] * (len(chunks[h]) + len(extra))
        more = {}
        if out is not None:
            more["input_output_aliases"] = {len(args): 0}
            args = (*args, out)
            in_specs = in_specs + [pl.BlockSpec(memory_space=pl.ANY)]
        heads = q_cols // head_dim
        out = call(
            functools.partial(attend_body, home_rows, homes, steps, h, is_early),
            shape((local_rows, q_cols * kv_here), BF16),
            args,
            in_specs=in_specs,
            out_specs=pl.BlockSpec((local_rows, q_cols), lambda i, h=h: (0, h)),
            grid=(1,),
            scratch=[pltpu.VMEM((heads * local_rows, head_dim), F32)] * 3,
            flops=4 * local_rows * heads * cached * head_dim,
            bytes_=4 * home_rows * cached * head_dim,
            **more,
        )
    return out.reshape(steps, home_rows, q_cols * kv_here).transpose(1, 0, 2)


def solution(mesh):
    return jax.shard_map(
        on_device,
        mesh=mesh,
        in_specs=(
            P("groups", None, "pool"),
            P("pool", ("tp", "sub")),
            P("pool", ("tp", "sub")),
            P("pool", ("tp", "sub")),
            P(("groups", "pool"), ("tp", "sub"), None, None),
            P(("groups", "pool"), ("tp", "sub"), None, None),
            P(("groups", "pool"), None, ("tp", "sub")),
            P(("groups", "pool"), None, ("tp", "sub")),
            P(("groups", "pool"), None, ("tp", "sub")),
            P("groups"),
            P("groups"),
            P("groups"),
        ),
        out_specs=P(("groups", "pool"), None, ("tp", "sub")),
        check_vma=False,
    )
```

```python
import functools
import math

import jax
import jax.numpy as jnp
from jax import lax
from jax.experimental import pallas as pl
from jax.experimental.pallas import tpu as pltpu
from jax.sharding import PartitionSpec as P

ROPE_BASE = 500000.0
BF16 = jnp.bfloat16
F32 = jnp.float32
FEATURE_AXES = ("tp", "sub")
CARRIER = ((0, 3, 2, 1), (2, 1, 0, 3), (3, 1, 2, 0), (1, 2, 0, 3))
VMEM_LIMIT = 48 * 1024 * 1024


def call(body, out_shape, args, in_specs=None, out_specs=None, grid=None, scratch=(), flops=0, bytes_=0, **more):
    whole = pl.BlockSpec(memory_space=pltpu.VMEM)
    kwargs = {} if grid is None else {"grid": grid}
    if in_specs is None:
        in_specs = [whole] * len(args)
    if out_specs is None:
        out_specs = jax.tree.map(lambda _: whole, out_shape)
    return pl.pallas_call(
        body,
        out_shape=out_shape,
        in_specs=in_specs,
        out_specs=out_specs,
        scratch_shapes=list(scratch),
        compiler_params=pltpu.CompilerParams(vmem_limit_bytes=VMEM_LIMIT),
        cost_estimate=pl.CostEstimate(flops=flops, bytes_accessed=bytes_, transcendentals=0),
        **kwargs,
        **more,
    )(*args)


VMEM = pl.BlockSpec(memory_space=pltpu.VMEM)
SMEM = pl.BlockSpec(memory_space=pltpu.SMEM)
HBM = pl.BlockSpec(memory_space=pltpu.HBM)
ANY = pl.BlockSpec(memory_space=pl.ANY)


def iota(shape, dim):
    return lax.broadcasted_iota(jnp.int32, shape, dim)


def nn(a, b):
    return lax.dot_general(a, b, (((1,), (0,)), ((), ())), preferred_element_type=F32)


def nt(a, b):
    return lax.dot_general(a, b, (((1,), (1,)), ((), ())), preferred_element_type=F32)


def tn(a, b):
    return lax.dot_general(a, b, (((0,), (0,)), ((), ())), preferred_element_type=F32)


def row_facts(row_request, request_adapter, lengths, home_rows, resident):
    rows = row_request.shape[1]
    across, down = iota((rows, rows), 1), iota((rows, rows), 0)
    eye = across == down
    request_col = jnp.sum(jnp.where(eye, row_request.astype(F32), 0.0), 1, keepdims=True)
    held = request_col == across.astype(F32)
    adapter_col = jnp.sum(jnp.where(held, request_adapter.astype(F32), 0.0), 1, keepdims=True)
    length_col = jnp.sum(jnp.where(held, lengths.astype(F32), 0.0), 1, keepdims=True)
    adapter_row = jnp.sum(jnp.where(eye, adapter_col, 0.0), 0, keepdims=True)
    length_row = jnp.sum(jnp.where(eye, length_col, 0.0), 0, keepdims=True)
    owner_col = jnp.floor((adapter_col + 0.5) / resident)
    owner_row = jnp.floor((adapter_row + 0.5) / resident)
    before = (owner_col == owner_row) & (down < across) & (down // home_rows == across // home_rows)
    slot_row = jnp.sum(jnp.where(before, 1.0, 0.0), 0, keepdims=True)
    return adapter_row, owner_row, slot_row, length_row


def slot_table(owner_row, slot_row, owner, home_rows, cap):
    rows = owner_row.shape[1]
    places = rows // home_rows * cap
    place, row = iota((places, rows), 0), iota((places, rows), 1)
    return (
        (owner_row == owner.astype(F32))
        & (place // cap == row // home_rows)
        & (slot_row == (place % cap).astype(F32))
    )


def select_body(home_rows, cap, resident, where_ref, rr_hbm, ra_hbm, ln_hbm, hid_hbm, *rest):
    outs, rest = rest[:-6], rest[-6:]
    facts_ref, rr_ref, ra_ref, ln_ref, hid_ref, sems = rest
    copies = [
        pltpu.make_async_copy(source, target, sems.at[n])
        for n, (source, target) in enumerate(
            ((rr_hbm, rr_ref), (ra_hbm, ra_ref), (ln_hbm, ln_ref), (hid_hbm, hid_ref))
        )
    ]
    for copy in copies:
        copy.start()
    for copy in copies[:3]:
        copy.wait()
    adapter_row, owner_row, slot_row, length_row = row_facts(
        rr_ref[...], ra_ref[...], ln_ref[...], home_rows, resident
    )
    facts_ref[...] = jnp.concatenate([adapter_row, owner_row, slot_row, length_row] * 2, 0)
    tables = [
        slot_table(owner_row, slot_row, where_ref[1 + i], home_rows, cap).astype(BF16) for i in range(len(outs))
    ]
    copies[3].wait()
    for table, out in zip(tables, outs):
        places = table.shape[0]
        for s in range(hid_ref.shape[0]):
            out[s * places : (s + 1) * places] = nn(table, hid_ref[s]).astype(BF16)


def project_body(home_rows, homes, early, late, where_ref, x_ref, q_ref, k_ref, v_ref, *rest):
    steps, rows = x_ref.shape[0] // (homes * home_rows), homes * home_rows
    tile = q_ref.shape[1]
    kv_heads = len(early) + len(late)
    head_dim = k_ref.shape[1] // kv_heads
    chunks, rest = rest[: homes * len(early)], rest[homes * len(early) :]
    whole, (scr, scr_kv) = rest[: len(late)], rest[len(late) :]
    i = pl.program_id(0)
    tiles = pl.num_programs(0) // kv_heads
    q_cols = tiles * tile
    columns = pl.ds(pl.multiple_of(lax.rem(i, tiles) * tile, tile), tile)

    def put(value, source, outs, where):
        source[...] = value
        for d in range(homes):
            home = where_ref[0] ^ d
            for s in range(steps):
                begin = pl.multiple_of(s * rows + home * home_rows, home_rows)
                outs[d][s * home_rows : (s + 1) * home_rows, where] = source[
                    pl.ds(begin, home_rows), :
                ].astype(BF16)

    for n, h in enumerate(early):

        @pl.when(i // tiles == h)
        def _(n=n):
            put(nn(x_ref[...], q_ref[...]), scr, chunks[n * homes : (n + 1) * homes], columns)

    for n, h in enumerate(late):

        @pl.when(i // tiles == h)
        def _(n=n):
            whole[n][:, columns] = nn(x_ref[...], q_ref[...])

    @pl.when(i == 0)
    def _():
        keys, values = nn(x_ref[...], k_ref[...]), nn(x_ref[...], v_ref[...])
        for h in range(kv_heads):
            here = slice(h * head_dim, (h + 1) * head_dim)
            both = jnp.concatenate([keys[:, here], values[:, here]], 1)
            if h in early:
                n = early.index(h)
                put(both, scr_kv, chunks[n * homes : (n + 1) * homes], slice(q_cols, q_cols + 2 * head_dim))
            else:
                whole[late.index(h)][:, q_cols:] = both


def shrink_body(home_rows, cap, resident, parts, where_ref, facts_ref, down_ref, *rest):
    sent, out = rest[:parts], rest[-1]
    adapter_row, owner_row, slot_row = facts_ref[0:1], facts_ref[1:2], facts_ref[2:3]
    me = where_ref[0]
    table = slot_table(owner_row, slot_row, me, home_rows, cap)
    local = jnp.sum(jnp.where(table, adapter_row - (me * resident).astype(F32) + 1.0, 0.0), 1, keepdims=True) - 1.0
    places = table.shape[0]
    steps = sent[0].shape[0] // places
    local = jnp.concatenate([local] * steps, 0)
    width = sent[0].shape[1]
    total = None
    for a in range(resident):
        term = None
        for i in range(parts):
            if parts == 1:
                block = down_ref[a]
            else:
                part = lax.rem(me + parts * places - i, parts)
                block = down_ref[a, :, pl.ds(pl.multiple_of(part * width, width), width)]
            piece = nt(sent[i][...], block)
            term = piece if term is None else term + piece
        term = jnp.where(local == float(a), term, 0.0)
        total = term if total is None else total + term
    out[...] = total.astype(BF16)


def expand_body(home_rows, homes, cap, resident, early, late, where_ref, facts_ref, upq_ref, upv_ref, *rest):
    n_parts = len(rest) - len(late) - homes * (len(early) + len(late)) - (1 if late else 0)
    shares, rest = rest[:n_parts], rest[n_parts:]
    partials, rest = rest[: len(late)], rest[len(late) :]
    early_outs, rest = rest[: homes * len(early)], rest[homes * len(early) :]
    late_outs, rest = rest[: homes * len(late)], rest[homes * len(late) :]
    adapter_row, owner_row, slot_row = facts_ref[0:1], facts_ref[1:2], facts_ref[2:3]
    me = where_ref[0]
    table = slot_table(owner_row, slot_row, me, home_rows, cap)
    places, rows = table.shape
    local = jnp.sum(jnp.where(table, adapter_row - (me * resident).astype(F32) + 1.0, 0.0), 1, keepdims=True) - 1.0
    spread = table.astype(BF16)
    shrunk = shares[0][...].astype(F32)
    for share in shares[1:]:
        shrunk = shrunk + share[...].astype(F32)
    steps = shrunk.shape[0] // places
    local = jnp.concatenate([local] * steps, 0)
    rank = upq_ref.shape[1]
    low_q, low_v = shrunk[:, :rank], shrunk[:, rank:]
    masked_q = [jnp.where(local == float(a), low_q, 0.0).astype(BF16) for a in range(resident)]
    masked_v = [jnp.where(local == float(a), low_v, 0.0).astype(BF16) for a in range(resident)]
    kv_heads = len(early) + len(late)
    width_q = upq_ref.shape[2] // kv_heads
    width_v = upv_ref.shape[2] // kv_heads

    def up(h):
        delta_q = delta_v = None
        for a in range(resident):
            term_q = nn(masked_q[a], upq_ref[a, :, h * width_q : (h + 1) * width_q])
            term_v = nn(masked_v[a], upv_ref[a, :, h * width_v : (h + 1) * width_v])
            delta_q = term_q if delta_q is None else delta_q + term_q
            delta_v = term_v if delta_v is None else delta_v + term_v
        return delta_q, delta_v

    for n, h in enumerate(early):
        both = jnp.concatenate(up(h), 1)
        scr = rest[-1]
        scr[: both.shape[0], : both.shape[1]] = both
        for d in range(homes):
            home = me ^ d
            pieces = []
            for s in range(steps):
                begin = pl.multiple_of(s * places + home * cap, cap)
                pieces.append(scr[pl.ds(begin, cap), : both.shape[1]])
            early_outs[n * homes + d][...] = jnp.concatenate(pieces, 0).astype(BF16)
    for n, h in enumerate(late):
        delta_q, delta_v = up(h)
        scr = rest[-1]
        for s in range(steps):
            here = slice(s * places, (s + 1) * places)
            there = slice(s * rows, (s + 1) * rows)
            scr[there, :width_q] = partials[n][there, :width_q] + tn(spread, delta_q[here].astype(BF16))
            scr[there, width_q : width_q + width_v] = partials[n][there, width_q : width_q + width_v]
            scr[there, width_q + width_v :] = partials[n][there, width_q + width_v :] + tn(
                spread, delta_v[here].astype(BF16)
            )
        for d in range(homes):
            home = me ^ d
            for s in range(steps):
                begin = pl.multiple_of(s * rows + home * home_rows, home_rows)
                late_outs[n * homes + d][s * home_rows : (s + 1) * home_rows, :] = scr[
                    pl.ds(begin, home_rows), :
                ].astype(BF16)


def home_body(home_rows, homes, cap, steps, where_ref, facts_ref, _, cos_ref, sin_ref, len_ref, *places_out):
    owner_row, slot_row, length_row = facts_ref[1:2], facts_ref[2:3], facts_ref[3:4]
    me = where_ref[0]
    local_rows, head_dim = cos_ref.shape
    rows = facts_ref.shape[1]
    row, batch = iota((local_rows, rows), 0), iota((local_rows, rows), 1)
    mine = batch == me * home_rows + row % home_rows
    length = jnp.sum(jnp.where(mine, length_row, 0.0), 1, keepdims=True)
    owner = jnp.sum(jnp.where(mine, owner_row, 0.0), 1, keepdims=True)
    slot = jnp.sum(jnp.where(mine, slot_row, 0.0), 1, keepdims=True)
    len_ref[...] = jnp.broadcast_to(length[:home_rows], len_ref.shape)
    lane = iota((local_rows, head_dim), 1)
    step = iota((local_rows, head_dim), 0) // home_rows
    half = head_dim // 2
    inverse_freq = jnp.exp((lane % half).astype(F32) * (-2.0 * math.log(ROPE_BASE) / head_dim))
    angle = (length + step.astype(F32)) * inverse_freq
    cos_ref[...] = jnp.cos(angle)
    sin_ref[...] = jnp.where(lane < half, -1.0, 1.0) * jnp.sin(angle)
    place, local = iota((local_rows, steps * cap), 1), iota((local_rows, steps * cap), 0)
    for d, out in enumerate(places_out):
        out[...] = (
            (owner == (me ^ d).astype(F32))
            & (place // cap == local // home_rows)
            & (slot == (place % cap).astype(F32))
        ).astype(BF16)


def attend_body(home_rows, homes, steps, h, early, cos_ref, sin_ref, len_ref, kc_ref, vc_ref, *rest):
    chunks, rest = rest[:homes], rest[homes:]
    places = deltas = ()
    if early:
        places, deltas, rest = rest[:homes], rest[homes : 2 * homes], rest[2 * homes :]
    done, (out, q_scr, new_scr, o_scr, total_scr) = rest[:-5], rest[-5:]
    local_rows, head_dim = cos_ref.shape
    cached = kc_ref.shape[2]
    heads = (chunks[0].shape[1] - 2 * head_dim) // head_dim
    width_q = heads * head_dim
    scale = 1.0 / math.sqrt(head_dim)
    cos, sin = cos_ref[...], sin_ref[...]

    def rope(v):
        return v * cos + pltpu.roll(v, head_dim // 2, 1) * sin

    def projected(begin, delta_begin):
        total = None
        for chunk in chunks:
            piece = chunk[:, begin : begin + head_dim].astype(F32)
            total = piece if total is None else total + piece
        if deltas and delta_begin is not None:
            delta = None
            for place, piece in zip(places, deltas):
                term = nn(place[...], piece[:, delta_begin : delta_begin + head_dim])
                delta = term if delta is None else delta + term
            total = total + delta
        return total

    key_new = rope(projected(width_q, None)).astype(BF16)
    value_new = projected(width_q + head_dim, width_q).astype(BF16)
    row, col = iota((local_rows, local_rows), 0), iota((local_rows, local_rows), 1)
    live = (row % home_rows == col % home_rows) & (col // home_rows <= row // home_rows)
    new_weights = []
    for n in range(heads):
        query = rope(projected(n * head_dim, n * head_dim)).astype(BF16)
        here = slice(n * local_rows, (n + 1) * local_rows)
        q_scr[here, :] = query.astype(F32)
        weight = jnp.where(live, jnp.exp(nt(query, key_new) * scale), 0.0)
        new_weights.append(weight)
        new_scr[here, :] = jnp.broadcast_to(jnp.sum(weight, 1, keepdims=True), (local_rows, head_dim))
    per_row = heads * steps
    spot = iota((per_row, cached), 1).astype(F32)
    mine = [pl.ds(b, per_row, stride=home_rows) for b in range(home_rows)]
    scores = [nt(q_scr[mine[b], :].astype(BF16), kc_ref[b, h]) for b in range(home_rows)]
    probs = []
    for b in range(home_rows):
        weight = jnp.where(spot < len_ref[b : b + 1, :], jnp.exp(scores[b] * scale), 0.0)
        total = jnp.sum(weight, 1, keepdims=True) + new_scr[mine[b], :][:, :1]
        total_scr[mine[b], :] = jnp.broadcast_to(total, (per_row, head_dim))
        probs.append((weight / total).astype(BF16))
    for b in range(home_rows):
        o_scr[mine[b], :] = nn(probs[b], vc_ref[b, h])
    begin = out.shape[1] - width_q
    for n in range(heads):
        here = slice(n * local_rows, (n + 1) * local_rows)
        prob = (new_weights[n] / total_scr[here, :local_rows]).astype(BF16)
        out[:, begin + n * head_dim : begin + (n + 1) * head_dim] = (
            o_scr[here, :] + nn(prob, value_new)
        ).astype(BF16)
    for n, piece in enumerate(done):
        out[:, n * width_q : (n + 1) * width_q] = piece[...]


def on_device(
    hidden,
    query_weight,
    key_weight,
    value_weight,
    key_cache_rows,
    value_cache_rows,
    adapter_down_weight,
    adapter_up_query,
    adapter_up_value,
    request_adapter,
    row_request,
    lengths,
):
    homes = lax.axis_size("pool")
    features = lax.axis_size(FEATURE_AXES)
    home_rows, kv_here, cached, head_dim = key_cache_rows.shape
    rows, steps, slice_width = hidden.shape
    resident = adapter_down_weight.shape[0]
    rank = adapter_up_query.shape[1]
    q_cols = query_weight.shape[1] // kv_here
    cap = max(2, 2 * home_rows // homes)
    places = homes * cap
    fold = homes // features
    local_rows = steps * home_rows
    width = q_cols + 2 * head_dim
    shape = jax.ShapeDtypeStruct

    pool_here = lax.axis_index("pool")
    feature_here = lax.axis_index(FEATURE_AXES)
    tuned = homes == len(CARRIER) and features == len(CARRIER)
    if tuned:
        targets = [[CARRIER[q].index(g) for g in range(features)] for q in range(homes)]
        target = sum(
            jnp.where((pool_here == q) & (feature_here == g), targets[q][g], 0)
            for q in range(homes)
            for g in range(features)
        )
        owners = [target]
        perms = [[(q * features + g, targets[q][g] * features + q) for q in range(homes) for g in range(features)]]
    else:
        owners = [feature_here * fold + (i + pool_here) % fold for i in range(fold)]
        perms = [
            [
                (q * features + g, (g * fold + (i + q) % fold) * features + q // fold)
                for q in range(homes)
                for g in range(features)
            ]
            for i in range(fold)
        ]
    where = jnp.stack([pool_here, *owners]).astype(jnp.int32)
    rr, ra, ln = row_request.reshape(1, rows), request_adapter.reshape(1, rows), lengths.reshape(1, rows)
    by_step = hidden.transpose(1, 0, 2)
    x = by_step.reshape(steps * rows, slice_width)
    early = tuple(range(kv_here // 2))
    late = tuple(range(kv_here // 2, kv_here))

    *selected, facts = call(
        functools.partial(select_body, home_rows, cap, resident),
        [shape((steps * places, slice_width), BF16)] * fold + [shape((8, rows), F32)],
        (where, rr, ra, ln, by_step),
        in_specs=[SMEM] + [HBM] * 4,
        scratch=[pltpu.VMEM((1, rows), jnp.int32)] * 3
        + [pltpu.VMEM(by_step.shape, BF16), pltpu.SemaphoreType.DMA((4,))],
        flops=2 * steps * places * rows * slice_width,
        bytes_=2 * steps * (rows + places) * slice_width,
    )
    sent = [lax.ppermute(s, ("pool", *FEATURE_AXES), perm) for s, perm in zip(selected, perms)]

    tile = min(256, q_cols)
    tiles = q_cols // tile
    project_shape = [shape((local_rows, width), BF16)] * (homes * len(early)) + [
        shape((steps * rows, width), F32)
    ] * len(late)
    projected = call(
        functools.partial(project_body, home_rows, homes, early, late),
        project_shape,
        (where, x, query_weight, key_weight, value_weight),
        in_specs=[
            SMEM,
            pl.BlockSpec(x.shape, lambda i: (0, 0)),
            pl.BlockSpec((slice_width, tile), lambda i: (0, i)),
            pl.BlockSpec(key_weight.shape, lambda i: (0, 0)),
            pl.BlockSpec(value_weight.shape, lambda i: (0, 0)),
        ],
        out_specs=[pl.BlockSpec(s.shape, lambda i: (0, 0)) for s in project_shape],
        grid=(tiles * kv_here,),
        scratch=[pltpu.VMEM((steps * rows, tile), F32), pltpu.VMEM((steps * rows, 2 * head_dim), F32)],
        flops=2 * steps * rows * slice_width * width * kv_here,
        bytes_=2 * slice_width * width * kv_here,
    )
    partials = projected[homes * len(early) :]

    def to_home(pieces):
        return [pieces[0]] + [
            lax.ppermute(pieces[d], "pool", [(i, i ^ d) for i in range(homes)]) for d in range(1, homes)
        ]

    chunks = {h: to_home(projected[n * homes : (n + 1) * homes]) for n, h in enumerate(early)}
    tables = call(
        functools.partial(home_body, home_rows, homes, cap, steps),
        [shape((local_rows, head_dim), F32)] * 2
        + [shape((home_rows, cached), F32)]
        + [shape((local_rows, steps * cap), BF16)] * homes,
        (where, facts, partials[0]),
        in_specs=[SMEM, VMEM, ANY],
        flops=10**7,
        bytes_=10**5,
    )
    cos, sin, length, spots = tables[0], tables[1], tables[2], tables[3:]

    share = call(
        functools.partial(shrink_body, home_rows, cap, resident, fold),
        shape((steps * places, 2 * rank), BF16),
        (where, facts, adapter_down_weight, *sent, partials[0]),
        in_specs=[SMEM] + [VMEM] * (2 + fold) + [ANY],
        flops=4 * steps * places * rank * slice_width * fold * resident,
        bytes_=4 * resident * rank * slice_width * fold,
    )
    shares = [share] + [
        lax.ppermute(share, FEATURE_AXES, [(i, i ^ d) for i in range(features)]) for d in range(1, features)
    ]
    grown = call(
        functools.partial(expand_body, home_rows, homes, cap, resident, early, late),
        [shape((steps * cap, q_cols + head_dim), BF16)] * (homes * len(early))
        + [shape((local_rows, width), BF16)] * (homes * len(late)),
        (where, facts, adapter_up_query, adapter_up_value, *shares, *partials),
        in_specs=[SMEM] + [VMEM] * (3 + len(shares) + len(partials)),
        scratch=[pltpu.VMEM((max(rows, places) * steps, width), F32)],
        flops=2 * steps * places * rank * resident * q_cols * kv_here,
        bytes_=2 * resident * rank * q_cols * kv_here,
    )
    deltas = {h: to_home(grown[n * homes : (n + 1) * homes]) for n, h in enumerate(early)}
    grown = grown[homes * len(early) :]
    for n, h in enumerate(late):
        chunks[h] = to_home(grown[n * homes : (n + 1) * homes])

    heads = q_cols // head_dim
    done = []
    for h in range(kv_here):
        extra = (*spots, *deltas[h]) if h in early else ()
        before = done if h == kv_here - 1 else []
        args = (cos, sin, length, key_cache_rows, value_cache_rows, *chunks[h], *extra, *before)
        done.append(
            call(
                functools.partial(attend_body, home_rows, homes, steps, h, h in early),
                shape((local_rows, q_cols * (1 + len(before))), BF16),
                args,
                scratch=[pltpu.VMEM((heads * local_rows, head_dim), F32)] * 4,
                flops=4 * local_rows * heads * cached * head_dim,
                bytes_=4 * home_rows * cached * head_dim,
            )
        )
    return done[-1].reshape(steps, home_rows, q_cols * kv_here).transpose(1, 0, 2)


def solution(mesh):
    return jax.shard_map(
        on_device,
        mesh=mesh,
        in_specs=(
            P("groups", None, "pool"),
            P("pool", ("tp", "sub")),
            P("pool", ("tp", "sub")),
            P("pool", ("tp", "sub")),
            P(("groups", "pool"), ("tp", "sub"), None, None),
            P(("groups", "pool"), ("tp", "sub"), None, None),
            P(("groups", "pool"), None, ("tp", "sub")),
            P(("groups", "pool"), None, ("tp", "sub")),
            P(("groups", "pool"), None, ("tp", "sub")),
            P("groups"),
            P("groups"),
            P("groups"),
        ),
        out_specs=P(("groups", "pool"), None, ("tp", "sub")),
        check_vma=False,
    )
```

```python
import functools
import math

import jax
import jax.numpy as jnp
from jax import lax
from jax.experimental import pallas as pl
from jax.experimental.pallas import tpu as pltpu
from jax.sharding import PartitionSpec as P

ROPE_BASE = 500000.0
BF16 = jnp.bfloat16
F32 = jnp.float32
FEATURE_AXES = ("tp", "sub")
CARRIER = ((0, 3, 2, 1), (2, 1, 0, 3), (3, 1, 2, 0), (1, 2, 0, 3))


def call(body, out_shape, args, in_specs=None, out_specs=None, grid=None, scratch=(), flops=0, bytes_=0, limit=40, **more):
    whole = pl.BlockSpec(memory_space=pltpu.VMEM)
    kwargs = {} if grid is None else {"grid": grid}
    if in_specs is None:
        in_specs = [whole] * len(args)
    if out_specs is None:
        out_specs = jax.tree.map(lambda _: whole, out_shape)
    inner = getattr(body, "func", body)
    return pl.pallas_call(
        body,
        name=inner.__name__,
        out_shape=out_shape,
        in_specs=in_specs,
        out_specs=out_specs,
        scratch_shapes=list(scratch),
        compiler_params=pltpu.CompilerParams(vmem_limit_bytes=limit * 1024 * 1024),
        cost_estimate=pl.CostEstimate(flops=flops, bytes_accessed=bytes_, transcendentals=0),
        **kwargs,
        **more,
    )(*args)


VMEM = pl.BlockSpec(memory_space=pltpu.VMEM)
SMEM = pl.BlockSpec(memory_space=pltpu.SMEM)
HBM = pl.BlockSpec(memory_space=pltpu.HBM)
ANY = pl.BlockSpec(memory_space=pl.ANY)


def iota(shape, dim):
    return lax.broadcasted_iota(jnp.int32, shape, dim)


def nn(a, b):
    return lax.dot_general(a, b, (((1,), (0,)), ((), ())), preferred_element_type=F32)


def nt(a, b):
    return lax.dot_general(a, b, (((1,), (1,)), ((), ())), preferred_element_type=F32)


def tn(a, b):
    return lax.dot_general(a, b, (((0,), (0,)), ((), ())), preferred_element_type=F32)


def row_facts(row_request, request_adapter, lengths, home_rows, resident):
    rows = row_request.shape[1]
    across, down = iota((rows, rows), 1), iota((rows, rows), 0)
    eye = across == down
    request_col = jnp.sum(jnp.where(eye, row_request.astype(F32), 0.0), 1, keepdims=True)
    held = request_col == across.astype(F32)
    adapter_col = jnp.sum(jnp.where(held, request_adapter.astype(F32), 0.0), 1, keepdims=True)
    length_col = jnp.sum(jnp.where(held, lengths.astype(F32), 0.0), 1, keepdims=True)
    adapter_row = jnp.sum(jnp.where(eye, adapter_col, 0.0), 0, keepdims=True)
    length_row = jnp.sum(jnp.where(eye, length_col, 0.0), 0, keepdims=True)
    owner_col = jnp.floor((adapter_col + 0.5) / resident)
    owner_row = jnp.floor((adapter_row + 0.5) / resident)
    before = (owner_col == owner_row) & (down < across) & (down // home_rows == across // home_rows)
    slot_row = jnp.sum(jnp.where(before, 1.0, 0.0), 0, keepdims=True)
    return adapter_row, owner_row, slot_row, length_row


def slot_table(owner_row, slot_row, owner, home_rows, cap):
    rows = owner_row.shape[1]
    places = rows // home_rows * cap
    place, row = iota((places, rows), 0), iota((places, rows), 1)
    return (
        (owner_row == owner.astype(F32))
        & (place // cap == row // home_rows)
        & (slot_row == (place % cap).astype(F32))
    )


def select_body(home_rows, cap, resident, owners, rr_hbm, ra_hbm, ln_hbm, hid_hbm, *rest):
    outs, rest = rest[:-6], rest[-6:]
    facts_ref, rr_ref, ra_ref, ln_ref, hid_ref, sems = rest
    copies = [
        pltpu.make_async_copy(source, target, sems.at[n])
        for n, (source, target) in enumerate(
            ((rr_hbm, rr_ref), (ra_hbm, ra_ref), (ln_hbm, ln_ref), (hid_hbm, hid_ref))
        )
    ]
    for copy in copies:
        copy.start()
    for copy in copies[:3]:
        copy.wait()
    adapter_row, owner_row, slot_row, length_row = row_facts(
        rr_ref[...], ra_ref[...], ln_ref[...], home_rows, resident
    )
    facts_ref[...] = jnp.concatenate([adapter_row, owner_row, slot_row, length_row] * 2, 0)
    tables = [
        slot_table(owner_row, slot_row, owner, home_rows, cap).astype(BF16) for owner in owners()
    ]
    copies[3].wait()
    for table, out in zip(tables, outs):
        places = table.shape[0]
        for s in range(hid_ref.shape[0]):
            out[s * places : (s + 1) * places] = nn(table, hid_ref[s]).astype(BF16)


def project_early_body(home_rows, homes, heads, x_ref, q_ref, k_ref, v_ref, near_ref, far_ref, scr):
    steps, rows = x_ref.shape[0] // (homes * home_rows), homes * home_rows
    q_cols = q_ref.shape[1]
    head_dim = k_ref.shape[1]
    me = lax.axis_index("pool")
    local_rows = steps * home_rows
    base = pl.program_id(0) * 2 * local_rows
    scr[:, :q_cols] = nn(x_ref[...], q_ref[...])
    scr[:, q_cols : q_cols + head_dim] = nn(x_ref[...], k_ref[...])
    scr[:, q_cols + head_dim :] = nn(x_ref[...], v_ref[...])
    for out, ds in ((far_ref, (1, 3)), (near_ref, (0, 2))):
        for n, d in enumerate(ds):
            for s in range(steps):
                begin = pl.multiple_of(s * rows + (me ^ d) * home_rows, home_rows)
                there = pl.multiple_of(base + n * local_rows + s * home_rows, home_rows)
                out[pl.ds(there, home_rows), :] = scr[pl.ds(begin, home_rows), :].astype(BF16)


def project_late_body(x_ref, q_ref, k_ref, v_ref, facts_ref, out, facts_out):
    q_cols = q_ref.shape[1]
    head_dim = k_ref.shape[1]
    facts_out[...] = facts_ref[...]
    out[0, :, :q_cols] = nn(x_ref[...], q_ref[...]).astype(BF16)
    out[0, :, q_cols : q_cols + head_dim] = nn(x_ref[...], k_ref[...]).astype(BF16)
    out[0, :, q_cols + head_dim :] = nn(x_ref[...], v_ref[...]).astype(BF16)


def pass_body(message_ref, _, out_ref):
    out_ref[...] = message_ref[...]


def add_body(heads, near_ref, got_ref, out_ref):
    rows = near_ref.shape[0] // (2 * heads)
    for n in range(heads):
        here = slice((2 * n + 1) * rows, (2 * n + 2) * rows)
        out_ref[n * rows : (n + 1) * rows, :] = (
            near_ref[here, :].astype(F32) + got_ref[here, :].astype(F32)
        ).astype(BF16)


def shrink_body(home_rows, cap, resident, parts, facts_ref, down_ref, *rest):
    sent, out = rest[:parts], rest[-1]
    adapter_row, owner_row, slot_row = facts_ref[0:1], facts_ref[1:2], facts_ref[2:3]
    me = lax.axis_index("pool")
    table = slot_table(owner_row, slot_row, me, home_rows, cap)
    local = jnp.sum(jnp.where(table, adapter_row - (me * resident).astype(F32) + 1.0, 0.0), 1, keepdims=True) - 1.0
    places = table.shape[0]
    steps = sent[0].shape[0] // places
    local = jnp.concatenate([local] * steps, 0)
    width = sent[0].shape[1]
    total = None
    for a in range(resident):
        term = None
        for i in range(parts):
            if parts == 1:
                block = down_ref[a]
            else:
                part = lax.rem(me + parts * places - i, parts)
                block = down_ref[a, :, pl.ds(pl.multiple_of(part * width, width), width)]
            piece = nt(sent[i][...], block)
            term = piece if term is None else term + piece
        term = jnp.where(local == float(a), term, 0.0)
        total = term if total is None else total + term
    out[...] = total.astype(BF16)


def expand_body(home_rows, homes, cap, resident, early, late, facts_ref, upq_ref, upv_ref, *rest):
    messages, rest, scr = rest[-1 - homes : -1], rest[: -1 - homes], rest[-1]
    shares, partials = rest[:-1], rest[-1]
    adapter_row, owner_row, slot_row = facts_ref[0:1], facts_ref[1:2], facts_ref[2:3]
    me = lax.axis_index("pool")
    table = slot_table(owner_row, slot_row, me, home_rows, cap)
    places, rows = table.shape
    local = jnp.sum(jnp.where(table, adapter_row - (me * resident).astype(F32) + 1.0, 0.0), 1, keepdims=True) - 1.0
    spread = table.astype(BF16)
    shrunk = shares[0][...].astype(F32)
    for share in shares[1:]:
        shrunk = shrunk + share[...].astype(F32)
    steps = shrunk.shape[0] // places
    local_rows = steps * home_rows
    local = jnp.concatenate([local] * steps, 0)
    rank = upq_ref.shape[1]
    low_q, low_v = shrunk[:, :rank], shrunk[:, rank:]
    masked_q = [jnp.where(local == float(a), low_q, 0.0).astype(BF16) for a in range(resident)]
    masked_v = [jnp.where(local == float(a), low_v, 0.0).astype(BF16) for a in range(resident)]
    kv_heads = len(early) + len(late)
    width_q = upq_ref.shape[2] // kv_heads
    width_v = upv_ref.shape[2] // kv_heads

    def up(h):
        delta_q = delta_v = None
        for a in range(resident):
            term_q = nn(masked_q[a], upq_ref[a, :, h * width_q : (h + 1) * width_q])
            term_v = nn(masked_v[a], upv_ref[a, :, h * width_v : (h + 1) * width_v])
            delta_q = term_q if delta_q is None else delta_q + term_q
            delta_v = term_v if delta_v is None else delta_v + term_v
        return delta_q, delta_v

    for n, h in enumerate(late):
        delta_q, delta_v = up(h)
        for s in range(steps):
            here = slice(s * places, (s + 1) * places)
            there = slice(s * rows, (s + 1) * rows)
            scr[there, :width_q] = partials[n, there, :width_q].astype(F32) + tn(spread, delta_q[here].astype(BF16))
            scr[there, width_q : width_q + width_v] = partials[n, there, width_q : width_q + width_v].astype(F32)
            scr[there, width_q + width_v :] = partials[n, there, width_q + width_v :].astype(F32) + tn(
                spread, delta_v[here].astype(BF16)
            )
        for d in range(homes):
            home = me ^ d
            for s in range(steps):
                begin = pl.multiple_of(s * rows + home * home_rows, home_rows)
                row = n * local_rows + s * home_rows
                messages[d][row : row + home_rows, :] = scr[pl.ds(begin, home_rows), :].astype(BF16)
    for n, h in enumerate(early):
        delta_q, delta_v = up(h)
        both = jnp.concatenate([delta_q, delta_v, jnp.zeros((steps * places, width_v), F32)], 1)
        scr[: steps * places, :] = both
        for d in range(homes):
            home = me ^ d
            pieces = []
            for s in range(steps):
                begin = pl.multiple_of(s * places + home * cap, cap)
                pieces.append(scr[pl.ds(begin, cap), :])
            row = len(late) * local_rows + n * steps * cap
            messages[d][row : row + steps * cap, :] = jnp.concatenate(pieces, 0).astype(BF16)


def home_body(home_rows, homes, cap, steps, facts_ref, cos_ref, sin_ref, len_ref, *places_out):
    owner_row, slot_row, length_row = facts_ref[1:2], facts_ref[2:3], facts_ref[3:4]
    me = lax.axis_index("pool")
    local_rows, head_dim = cos_ref.shape
    rows = facts_ref.shape[1]
    row, batch = iota((local_rows, rows), 0), iota((local_rows, rows), 1)
    mine = batch == me * home_rows + row % home_rows
    length = jnp.sum(jnp.where(mine, length_row, 0.0), 1, keepdims=True)
    owner = jnp.sum(jnp.where(mine, owner_row, 0.0), 1, keepdims=True)
    slot = jnp.sum(jnp.where(mine, slot_row, 0.0), 1, keepdims=True)
    len_ref[...] = jnp.broadcast_to(length[:home_rows], len_ref.shape)
    lane = iota((local_rows, head_dim), 1)
    step = iota((local_rows, head_dim), 0) // home_rows
    half = head_dim // 2
    inverse_freq = jnp.exp((lane % half).astype(F32) * (-2.0 * math.log(ROPE_BASE) / head_dim))
    angle = (length + step.astype(F32)) * inverse_freq
    cos_ref[...] = jnp.cos(angle)
    sin_ref[...] = jnp.where(lane < half, -1.0, 1.0) * jnp.sin(angle)
    place, local = iota((local_rows, steps * cap), 1), iota((local_rows, steps * cap), 0)
    for d, out in enumerate(places_out):
        out[...] = (
            (owner == (me ^ d).astype(F32))
            & (place // cap == local // home_rows)
            & (slot == (place % cap).astype(F32))
        ).astype(BF16)


def attend_body(home_rows, homes, steps, early, late, cos_ref, sin_ref, len_ref, kc_ref, vc_ref, *rest):
    spots, rest = rest[: homes if early else 0], rest[homes if early else 0 :]
    early_sums, rest = rest[: 3 if early else 0], rest[3 if early else 0 :]
    messages, (out, q_scr, new_scr, o_scr, total_scr) = rest[:homes], rest[homes:]
    local_rows, head_dim = cos_ref.shape
    cached = kc_ref.shape[2]
    heads = (messages[0].shape[1] - 2 * head_dim) // head_dim
    width_q = heads * head_dim
    places = (messages[0].shape[0] - local_rows * len(late)) // max(1, len(early))
    scale = 1.0 / math.sqrt(head_dim)
    cos, sin = cos_ref[...], sin_ref[...]
    kv_heads = len(early) + len(late)

    def rope(v):
        return v * cos + pltpu.roll(v, head_dim // 2, 1) * sin

    def projected(h, begin, delta_begin):
        columns = slice(begin, begin + head_dim)
        if h in late:
            row = late.index(h) * local_rows
            pieces = [m[row : row + local_rows, columns] for m in messages]
        else:
            n = early.index(h)
            near, got, far_sum = early_sums
            here = slice(2 * n * local_rows, (2 * n + 1) * local_rows)
            pieces = [near[here, columns], got[here, columns], far_sum[n * local_rows : (n + 1) * local_rows, columns]]
        total = sum(piece.astype(F32) for piece in pieces)
        if h in early and delta_begin is not None:
            row = len(late) * local_rows + early.index(h) * places
            columns = slice(delta_begin, delta_begin + head_dim)
            total = total + sum(nn(spot[...], m[row : row + places, columns]) for spot, m in zip(spots, messages))
        return total

    row, col = iota((local_rows, local_rows), 0), iota((local_rows, local_rows), 1)
    live = (row % home_rows == col % home_rows) & (col // home_rows <= row // home_rows)
    per_row = heads * steps
    spot_ids = iota((per_row, cached), 1).astype(F32)
    every = [(h, b) for h in range(kv_heads) for b in range(home_rows)]
    mine = {
        (h, b): pl.ds(h * heads * local_rows + b, per_row, stride=home_rows) for h, b in every
    }
    new_weights, values_new = {}, {}
    for h in range(kv_heads):
        key_new = rope(projected(h, width_q, None)).astype(BF16)
        values_new[h] = projected(h, width_q + head_dim, width_q).astype(BF16)
        for n in range(heads):
            query = rope(projected(h, n * head_dim, n * head_dim)).astype(BF16)
            here = slice((h * heads + n) * local_rows, (h * heads + n + 1) * local_rows)
            q_scr[here, :] = query.astype(F32)
            weight = jnp.where(live, jnp.exp(nt(query, key_new) * scale), 0.0)
            new_weights[h, n] = weight
            new_scr[here, :] = jnp.broadcast_to(jnp.sum(weight, 1, keepdims=True), (local_rows, head_dim))
    for h in range(kv_heads):
        scores = [nt(q_scr[mine[h, b], :].astype(BF16), kc_ref[b, h]) for b in range(home_rows)]
        probs = []
        for b in range(home_rows):
            weight = jnp.where(spot_ids < len_ref[b : b + 1, :], jnp.exp(scores[b] * scale), 0.0)
            total = jnp.sum(weight, 1, keepdims=True) + new_scr[mine[h, b], :][:, :1]
            total_scr[mine[h, b], :] = jnp.broadcast_to(total, (per_row, head_dim))
            probs.append((weight / total).astype(BF16))
        for b in range(home_rows):
            o_scr[mine[h, b], :] = nn(probs[b], vc_ref[b, h])
    for h in range(kv_heads):
        for n in range(heads):
            at = h * heads + n
            here = slice(at * local_rows, (at + 1) * local_rows)
            prob = (new_weights[h, n] / total_scr[here, :local_rows]).astype(BF16)
            out[:, at * head_dim : (at + 1) * head_dim] = (
                o_scr[here, :] + nn(prob, values_new[h])
            ).astype(BF16)


def on_device(
    hidden,
    query_weight,
    key_weight,
    value_weight,
    key_cache_rows,
    value_cache_rows,
    adapter_down_weight,
    adapter_up_query,
    adapter_up_value,
    request_adapter,
    row_request,
    lengths,
):
    homes = lax.axis_size("pool")
    features = lax.axis_size(FEATURE_AXES)
    home_rows, kv_here, cached, head_dim = key_cache_rows.shape
    rows, steps, slice_width = hidden.shape
    resident = adapter_down_weight.shape[0]
    rank = adapter_up_query.shape[1]
    q_cols = query_weight.shape[1] // kv_here
    cap = max(2, 2 * home_rows // homes)
    places = homes * cap
    fold = homes // features
    local_rows = steps * home_rows
    width = q_cols + 2 * head_dim
    shape = jax.ShapeDtypeStruct

    if homes == len(CARRIER) and features == len(CARRIER):
        targets = [[CARRIER[q].index(g) for g in range(features)] for q in range(homes)]
        perms = [[(q * features + g, targets[q][g] * features + q) for q in range(homes) for g in range(features)]]

        def owners():
            pool_here, feature_here = lax.axis_index("pool"), lax.axis_index(FEATURE_AXES)
            at = pool_here * features + feature_here
            owner = jnp.int32(0)
            for q in range(homes):
                for g in range(features):
                    owner = jnp.where(at == q * features + g, targets[q][g], owner)
            return [owner]

    else:
        perms = [
            [
                (q * features + g, (g * fold + (i + q) % fold) * features + q // fold)
                for q in range(homes)
                for g in range(features)
            ]
            for i in range(fold)
        ]

        def owners():
            pool_here, feature_here = lax.axis_index("pool"), lax.axis_index(FEATURE_AXES)
            return [feature_here * fold + lax.rem(pool_here + i, fold) for i in range(fold)]

    rr, ra, ln = row_request.reshape(1, rows), request_adapter.reshape(1, rows), lengths.reshape(1, rows)
    by_step = hidden.transpose(1, 0, 2)
    x = by_step.reshape(steps * rows, slice_width)
    early = ()
    late = tuple(range(kv_here))

    *selected, facts = call(
        functools.partial(select_body, home_rows, cap, resident, owners),
        [shape((steps * places, slice_width), BF16)] * fold + [shape((8, rows), F32)],
        (rr, ra, ln, by_step),
        in_specs=[HBM] * 4,
        limit=60,
        scratch=[pltpu.VMEM((1, rows), jnp.int32)] * 3
        + [pltpu.VMEM(by_step.shape, BF16), pltpu.SemaphoreType.DMA((4,))],
        flops=2 * steps * places * rows * slice_width,
        bytes_=2 * steps * (rows + places) * slice_width,
    )
    sent = [lax.ppermute(s, ("pool", *FEATURE_AXES), perm) for s, perm in zip(selected, perms)]

    def swap(value, d):
        return lax.ppermute(value, "pool", [(i, i ^ d) for i in range(homes)])

    weights = (x, query_weight, key_weight, value_weight)

    def weight_specs(first):
        return [
            pl.BlockSpec(x.shape, lambda i: (0, 0)),
            pl.BlockSpec((slice_width, q_cols), lambda i: (0, first + i)),
            pl.BlockSpec((slice_width, head_dim), lambda i: (0, first + i)),
            pl.BlockSpec((slice_width, head_dim), lambda i: (0, first + i)),
        ]

    early_sums = ()
    if early:
        pair = shape((2 * local_rows * len(early), width), BF16)
        near, far = call(
            functools.partial(project_early_body, home_rows, homes, len(early)),
            [pair] * 2,
            weights,
            limit=60,
            in_specs=weight_specs(0),
            out_specs=[pl.BlockSpec(pair.shape, lambda i: (0, 0))] * 2,
            grid=(len(early),),
            scratch=[pltpu.VMEM((steps * rows, width), F32)],
            flops=2 * steps * rows * slice_width * width * len(early),
            bytes_=2 * slice_width * width * len(early),
        )
        got = swap(far, 1)

    partials, facts = call(
        project_late_body,
        [shape((kv_here, steps * rows, width), BF16), shape(facts.shape, F32)],
        (*weights, facts),
        in_specs=weight_specs(0) + [pl.BlockSpec(facts.shape, lambda i: (0, 0))],
        out_specs=[
            pl.BlockSpec((1, steps * rows, width), lambda i: (i, 0, 0)),
            pl.BlockSpec(facts.shape, lambda i: (0, 0)),
        ],
        grid=(kv_here,),
        limit=50,
        flops=2 * steps * rows * slice_width * width * kv_here,
        bytes_=2 * slice_width * width * kv_here,
    )
    share = call(
        functools.partial(shrink_body, home_rows, cap, resident, fold),
        shape((steps * places, 2 * rank), BF16),
        (facts, adapter_down_weight, *sent),
        flops=4 * steps * places * rank * slice_width * fold * resident,
        bytes_=4 * resident * rank * slice_width * fold,
    )
    shares = [share] + [
        lax.ppermute(share, FEATURE_AXES, [(i, i ^ d) for i in range(features)]) for d in range(1, features)
    ]
    tables = call(
        functools.partial(home_body, home_rows, homes, cap, steps),
        [shape((local_rows, head_dim), F32)] * 2
        + [shape((home_rows, cached), F32)]
        + [shape((local_rows, steps * cap), BF16)] * homes,
        (facts,),
        flops=10**7,
        bytes_=10**5,
    )
    cos, sin, length, spots = tables[0], tables[1], tables[2], tables[3:]
    if early:
        far_sum = call(
            functools.partial(add_body, len(early)),
            shape((local_rows * len(early), width), BF16),
            (near, got),
            flops=local_rows * len(early) * width,
            bytes_=6 * local_rows * len(early) * width,
        )
        early_sums = (near, got, swap(far_sum, 2))
    message = shape((local_rows * len(late) + steps * cap * len(early), width), BF16)
    messages = call(
            functools.partial(expand_body, home_rows, homes, cap, resident, early, late),
            [message] * homes,
            (facts, adapter_up_query, adapter_up_value, *shares, partials),
                        scratch=[pltpu.VMEM((max(rows, places) * steps, width), F32)],
            flops=2 * steps * places * rank * resident * q_cols * kv_here,
            bytes_=2 * resident * rank * q_cols * kv_here,
        )
    messages = list(messages)
    if early:
        messages[1] = call(pass_body, message, (messages[1], early_sums[2]), in_specs=[VMEM, ANY])
    messages = [messages[0]] + [swap(messages[d], d) for d in range(1, homes)]
    out = call(
        functools.partial(attend_body, home_rows, homes, steps, early, late),
        shape((local_rows, q_cols * kv_here), BF16),
        (
            cos,
            sin,
            length,
            key_cache_rows,
            value_cache_rows,
            *(spots if early else ()),
            *early_sums,
            *messages,
        ),
        scratch=[pltpu.VMEM((kv_here * q_cols // head_dim * local_rows, head_dim), F32)] * 4,
        flops=4 * local_rows * q_cols * kv_here * cached,
        bytes_=4 * home_rows * cached * head_dim * kv_here,
    )
    return out.reshape(steps, home_rows, q_cols * kv_here).transpose(1, 0, 2)


def solution(mesh):
    return jax.shard_map(
        on_device,
        mesh=mesh,
        in_specs=(
            P("groups", None, "pool"),
            P("pool", ("tp", "sub")),
            P("pool", ("tp", "sub")),
            P("pool", ("tp", "sub")),
            P(("groups", "pool"), ("tp", "sub"), None, None),
            P(("groups", "pool"), ("tp", "sub"), None, None),
            P(("groups", "pool"), None, ("tp", "sub")),
            P(("groups", "pool"), None, ("tp", "sub")),
            P(("groups", "pool"), None, ("tp", "sub")),
            P("groups"),
            P("groups"),
            P("groups"),
        ),
        out_specs=P(("groups", "pool"), None, ("tp", "sub")),
        check_vma=False,
    )
```

```python
import functools
import math

import jax
import jax.numpy as jnp
from jax import lax
from jax.experimental import pallas as pl
from jax.experimental.pallas import tpu as pltpu
from jax.sharding import PartitionSpec as P

ROPE_BASE = 500000.0
BF16 = jnp.bfloat16
F32 = jnp.float32
FEATURE_AXES = ("tp", "sub")
CARRIER = ((0, 3, 2, 1), (2, 1, 0, 3), (3, 1, 2, 0), (1, 2, 0, 3))


def call(body, out_shape, args, in_specs=None, out_specs=None, grid=None, scratch=(), flops=0, bytes_=0, limit=40, **more):
    whole = pl.BlockSpec(memory_space=pltpu.VMEM)
    kwargs = {} if grid is None else {"grid": grid}
    if in_specs is None:
        in_specs = [whole] * len(args)
    if out_specs is None:
        out_specs = jax.tree.map(lambda _: whole, out_shape)
    inner = getattr(body, "func", body)
    return pl.pallas_call(
        body,
        name=inner.__name__,
        out_shape=out_shape,
        in_specs=in_specs,
        out_specs=out_specs,
        scratch_shapes=list(scratch),
        compiler_params=pltpu.CompilerParams(vmem_limit_bytes=limit * 1024 * 1024),
        cost_estimate=pl.CostEstimate(flops=flops, bytes_accessed=bytes_, transcendentals=0),
        **kwargs,
        **more,
    )(*args)


VMEM = pl.BlockSpec(memory_space=pltpu.VMEM)
SMEM = pl.BlockSpec(memory_space=pltpu.SMEM)
HBM = pl.BlockSpec(memory_space=pltpu.HBM)
ANY = pl.BlockSpec(memory_space=pl.ANY)


def iota(shape, dim):
    return lax.broadcasted_iota(jnp.int32, shape, dim)


def nn(a, b):
    return lax.dot_general(a, b, (((1,), (0,)), ((), ())), preferred_element_type=F32)


def nt(a, b):
    return lax.dot_general(a, b, (((1,), (1,)), ((), ())), preferred_element_type=F32)


def tn(a, b):
    return lax.dot_general(a, b, (((0,), (0,)), ((), ())), preferred_element_type=F32)


def row_facts(row_request, request_adapter, lengths, home_rows, resident):
    rows = row_request.shape[1]
    across, down = iota((rows, rows), 1), iota((rows, rows), 0)
    eye = across == down
    request_col = jnp.sum(jnp.where(eye, row_request.astype(F32), 0.0), 1, keepdims=True)
    held = request_col == across.astype(F32)
    adapter_col = jnp.sum(jnp.where(held, request_adapter.astype(F32), 0.0), 1, keepdims=True)
    length_col = jnp.sum(jnp.where(held, lengths.astype(F32), 0.0), 1, keepdims=True)
    adapter_row = jnp.sum(jnp.where(eye, adapter_col, 0.0), 0, keepdims=True)
    length_row = jnp.sum(jnp.where(eye, length_col, 0.0), 0, keepdims=True)
    owner_col = jnp.floor((adapter_col + 0.5) / resident)
    owner_row = jnp.floor((adapter_row + 0.5) / resident)
    before = (owner_col == owner_row) & (down < across) & (down // home_rows == across // home_rows)
    slot_row = jnp.sum(jnp.where(before, 1.0, 0.0), 0, keepdims=True)
    return adapter_row, owner_row, slot_row, length_row


def slot_table(owner_row, slot_row, owner, home_rows, cap):
    rows = owner_row.shape[1]
    places = rows // home_rows * cap
    place, row = iota((places, rows), 0), iota((places, rows), 1)
    return (
        (owner_row == owner.astype(F32))
        & (place // cap == row // home_rows)
        & (slot_row == (place % cap).astype(F32))
    )


def select_body(home_rows, cap, resident, owners, rr_hbm, ra_hbm, ln_hbm, hid_hbm, *rest):
    outs, rest = rest[:-6], rest[-6:]
    facts_ref, rr_ref, ra_ref, ln_ref, hid_ref, sems = rest
    copies = [
        pltpu.make_async_copy(source, target, sems.at[n])
        for n, (source, target) in enumerate(
            ((rr_hbm, rr_ref), (ra_hbm, ra_ref), (ln_hbm, ln_ref), (hid_hbm, hid_ref))
        )
    ]
    for copy in copies:
        copy.start()
    for copy in copies[:3]:
        copy.wait()
    adapter_row, owner_row, slot_row, length_row = row_facts(
        rr_ref[...], ra_ref[...], ln_ref[...], home_rows, resident
    )
    facts_ref[...] = jnp.concatenate([adapter_row, owner_row, slot_row, length_row] * 2, 0)
    tables = [
        slot_table(owner_row, slot_row, owner, home_rows, cap).astype(BF16) for owner in owners()
    ]
    copies[3].wait()
    for table, out in zip(tables, outs):
        places = table.shape[0]
        for s in range(hid_ref.shape[0]):
            out[s * places : (s + 1) * places] = nn(table, hid_ref[s]).astype(BF16)


def project_body(x_ref, q_ref, k_ref, v_ref, facts_ref, out, facts_out):
    q_cols = q_ref.shape[1]
    head_dim = k_ref.shape[1]
    facts_out[...] = facts_ref[...]
    out[0, :, :q_cols] = nn(x_ref[...], q_ref[...]).astype(BF16)
    out[0, :, q_cols : q_cols + head_dim] = nn(x_ref[...], k_ref[...]).astype(BF16)
    out[0, :, q_cols + head_dim :] = nn(x_ref[...], v_ref[...]).astype(BF16)


def pass_body(message_ref, _, out_ref):
    out_ref[...] = message_ref[...]


def add_body(near_ref, got_ref, out_ref):
    rows = near_ref.shape[1] // 2
    out_ref[...] = (near_ref[:, rows:].astype(F32) + got_ref[:, rows:].astype(F32)).astype(BF16)


def shrink_body(home_rows, cap, resident, parts, facts_ref, down_ref, *rest):
    sent, out = rest[:parts], rest[-1]
    adapter_row, owner_row, slot_row = facts_ref[0:1], facts_ref[1:2], facts_ref[2:3]
    me = lax.axis_index("pool")
    table = slot_table(owner_row, slot_row, me, home_rows, cap)
    local = jnp.sum(jnp.where(table, adapter_row - (me * resident).astype(F32) + 1.0, 0.0), 1, keepdims=True) - 1.0
    places = table.shape[0]
    steps = sent[0].shape[0] // places
    local = jnp.concatenate([local] * steps, 0)
    width = sent[0].shape[1]
    total = None
    for a in range(resident):
        term = None
        for i in range(parts):
            if parts == 1:
                block = down_ref[a]
            else:
                part = lax.rem(me + parts * places - i, parts)
                block = down_ref[a, :, pl.ds(pl.multiple_of(part * width, width), width)]
            piece = nt(sent[i][...], block)
            term = piece if term is None else term + piece
        term = jnp.where(local == float(a), term, 0.0)
        total = term if total is None else total + term
    out[...] = total.astype(BF16)


def expand_body(home_rows, homes, heads, paired, features, facts_ref, upq_ref, upv_ref, *rest):
    shares, partials, outs, scr = rest[:features], rest[features], rest[-1 - (2 if paired else homes) : -1], rest[-1]
    adapter_row, owner_row, slot_row = facts_ref[0:1], facts_ref[1:2], facts_ref[2:3]
    me = lax.axis_index("pool")
    resident, rank = upq_ref.shape[:2]
    kv_heads, all_rows, width = partials.shape
    rows = owner_row.shape[1]
    steps = all_rows // rows
    local_rows = steps * home_rows
    shrunk = shares[0][...].astype(F32)
    for share in shares[1:]:
        shrunk = shrunk + share[...].astype(F32)
    places = shrunk.shape[0] // steps
    table = slot_table(owner_row, slot_row, me, home_rows, places // homes)
    local = jnp.sum(jnp.where(table, adapter_row - (me * resident).astype(F32) + 1.0, 0.0), 1, keepdims=True) - 1.0
    spread = table.astype(BF16)
    local = jnp.concatenate([local] * steps, 0)
    low_q, low_v = shrunk[:, :rank], shrunk[:, rank:]
    masked_q = [jnp.where(local == float(a), low_q, 0.0).astype(BF16) for a in range(resident)]
    masked_v = [jnp.where(local == float(a), low_v, 0.0).astype(BF16) for a in range(resident)]
    width_q = upq_ref.shape[2] // kv_heads
    width_v = upv_ref.shape[2] // kv_heads
    for at, h in enumerate(heads):
        delta_q = delta_v = 0.0
        for a in range(resident):
            delta_q = delta_q + nn(masked_q[a], upq_ref[a, :, h * width_q : (h + 1) * width_q])
            delta_v = delta_v + nn(masked_v[a], upv_ref[a, :, h * width_v : (h + 1) * width_v])
        for s in range(steps):
            here = slice(s * places, (s + 1) * places)
            there = slice(s * rows, (s + 1) * rows)
            middle, end = width_q, width_q + width_v
            scr[there, :middle] = partials[h, there, :middle].astype(F32) + tn(spread, delta_q[here].astype(BF16))
            scr[there, middle:end] = partials[h, there, middle:end].astype(F32)
            scr[there, end:] = partials[h, there, end:].astype(F32) + tn(spread, delta_v[here].astype(BF16))
        for d in range(homes):
            for s in range(steps):
                begin = pl.multiple_of(s * rows + (me ^ d) * home_rows, home_rows)
                row = s * home_rows + (d // 2 * local_rows if paired else 0)
                out = outs[d % 2] if paired else outs[d]
                out[at, row : row + home_rows, :] = scr[pl.ds(begin, home_rows), :].astype(BF16)


def home_body(home_rows, facts_ref, cos_ref, sin_ref, len_ref):
    length_row = facts_ref[3:4]
    me = lax.axis_index("pool")
    local_rows, head_dim = cos_ref.shape
    rows = facts_ref.shape[1]
    row, batch = iota((local_rows, rows), 0), iota((local_rows, rows), 1)
    mine = batch == me * home_rows + row % home_rows
    length = jnp.sum(jnp.where(mine, length_row, 0.0), 1, keepdims=True)
    len_ref[...] = jnp.broadcast_to(length[:home_rows], len_ref.shape)
    lane = iota((local_rows, head_dim), 1)
    step = iota((local_rows, head_dim), 0) // home_rows
    half = head_dim // 2
    inverse_freq = jnp.exp((lane % half).astype(F32) * (-2.0 * math.log(ROPE_BASE) / head_dim))
    angle = (length + step.astype(F32)) * inverse_freq
    cos_ref[...] = jnp.cos(angle)
    sin_ref[...] = jnp.where(lane < half, -1.0, 1.0) * jnp.sin(angle)


def attend_body(home_rows, which, n_pieces, cos_ref, sin_ref, len_ref, kc_ref, vc_ref, *rest):
    pieces, done, (out, q_scr, new_scr, o_scr, total_scr) = rest[:n_pieces], rest[n_pieces:-5], rest[-5:]
    local_rows, head_dim = cos_ref.shape
    steps = local_rows // home_rows
    cached = kc_ref.shape[2]
    kv_heads = len(which)
    heads = q_scr.shape[0] // (kv_heads * local_rows)
    width_q = heads * head_dim
    scale = 1.0 / math.sqrt(head_dim)
    cos, sin = cos_ref[...], sin_ref[...]

    def rope(v):
        return v * cos + pltpu.roll(v, head_dim // 2, 1) * sin

    def projected(h, begin):
        return sum(piece[h, :local_rows, begin : begin + head_dim].astype(F32) for piece in pieces)

    row, col = iota((local_rows, local_rows), 0), iota((local_rows, local_rows), 1)
    live = (row % home_rows == col % home_rows) & (col // home_rows <= row // home_rows)
    per_row = heads * steps
    spot_ids = iota((per_row, cached), 1).astype(F32)
    every = [(h, b) for h in range(kv_heads) for b in range(home_rows)]
    mine = {
        (h, b): pl.ds(h * heads * local_rows + b, per_row, stride=home_rows) for h, b in every
    }
    new_weights, values_new = {}, {}
    for h in range(kv_heads):
        key_new = rope(projected(h, width_q)).astype(BF16)
        values_new[h] = projected(h, width_q + head_dim).astype(BF16)
        for n in range(heads):
            query = rope(projected(h, n * head_dim)).astype(BF16)
            here = slice((h * heads + n) * local_rows, (h * heads + n + 1) * local_rows)
            q_scr[here, :] = query.astype(F32)
            weight = jnp.where(live, jnp.exp(nt(query, key_new) * scale), 0.0)
            new_weights[h, n] = weight
            new_scr[here, :] = jnp.broadcast_to(jnp.sum(weight, 1, keepdims=True), (local_rows, head_dim))
    for h in range(kv_heads):
        scores = [nt(q_scr[mine[h, b], :].astype(BF16), kc_ref[b, which[h]]) for b in range(home_rows)]
        probs = []
        for b in range(home_rows):
            weight = jnp.where(spot_ids < len_ref[b : b + 1, :], jnp.exp(scores[b] * scale), 0.0)
            total = jnp.sum(weight, 1, keepdims=True) + new_scr[mine[h, b], :][:, :1]
            total_scr[mine[h, b], :] = jnp.broadcast_to(total, (per_row, head_dim))
            probs.append((weight / total).astype(BF16))
        for b in range(home_rows):
            o_scr[mine[h, b], :] = nn(probs[b], vc_ref[b, which[h]])
    for h in range(kv_heads):
        for n in range(heads):
            at = h * heads + n
            here = slice(at * local_rows, (at + 1) * local_rows)
            prob = (new_weights[h, n] / total_scr[here, :local_rows]).astype(BF16)
            out[:, at * head_dim : (at + 1) * head_dim] = (
                o_scr[here, :] + nn(prob, values_new[h])
            ).astype(BF16)
    for piece in done:
        out[:, kv_heads * width_q :] = piece[...]


def on_device(
    hidden,
    query_weight,
    key_weight,
    value_weight,
    key_cache_rows,
    value_cache_rows,
    adapter_down_weight,
    adapter_up_query,
    adapter_up_value,
    request_adapter,
    row_request,
    lengths,
):
    homes = lax.axis_size("pool")
    features = lax.axis_size(FEATURE_AXES)
    home_rows, kv_here, cached, head_dim = key_cache_rows.shape
    rows, steps, slice_width = hidden.shape
    resident = adapter_down_weight.shape[0]
    rank = adapter_up_query.shape[1]
    q_cols = query_weight.shape[1] // kv_here
    cap = max(2, 2 * home_rows // homes)
    places = homes * cap
    fold = homes // features
    local_rows = steps * home_rows
    width = q_cols + 2 * head_dim
    shape = jax.ShapeDtypeStruct

    if homes == len(CARRIER) and features == len(CARRIER):
        targets = [[CARRIER[q].index(g) for g in range(features)] for q in range(homes)]
        perms = [[(q * features + g, targets[q][g] * features + q) for q in range(homes) for g in range(features)]]

        def owners():
            pool_here, feature_here = lax.axis_index("pool"), lax.axis_index(FEATURE_AXES)
            at = pool_here * features + feature_here
            owner = jnp.int32(0)
            for q in range(homes):
                for g in range(features):
                    owner = jnp.where(at == q * features + g, targets[q][g], owner)
            return [owner]

    else:
        perms = [
            [
                (q * features + g, (g * fold + (i + q) % fold) * features + q // fold)
                for q in range(homes)
                for g in range(features)
            ]
            for i in range(fold)
        ]

        def owners():
            pool_here, feature_here = lax.axis_index("pool"), lax.axis_index(FEATURE_AXES)
            return [feature_here * fold + lax.rem(pool_here + i, fold) for i in range(fold)]

    rr, ra, ln = row_request.reshape(1, rows), request_adapter.reshape(1, rows), lengths.reshape(1, rows)
    by_step = hidden.transpose(1, 0, 2)
    x = by_step.reshape(steps * rows, slice_width)
    halved = kv_here // 2 if homes == 4 else 0

    *selected, facts = call(
        functools.partial(select_body, home_rows, cap, resident, owners),
        [shape((steps * places, slice_width), BF16)] * fold + [shape((8, rows), F32)],
        (rr, ra, ln, by_step),
        in_specs=[HBM] * 4,
        limit=60,
        scratch=[pltpu.VMEM((1, rows), jnp.int32)] * 3
        + [pltpu.VMEM(by_step.shape, BF16), pltpu.SemaphoreType.DMA((4,))],
        flops=2 * steps * places * rows * slice_width,
        bytes_=2 * steps * (rows + places) * slice_width,
    )
    sent = [lax.ppermute(s, ("pool", *FEATURE_AXES), perm) for s, perm in zip(selected, perms)]

    def swap(value, d):
        return lax.ppermute(value, "pool", [(i, i ^ d) for i in range(homes)])

    weights = (x, query_weight, key_weight, value_weight)

    def weight_specs(first):
        return [
            pl.BlockSpec(x.shape, lambda i: (0, 0)),
            pl.BlockSpec((slice_width, q_cols), lambda i: (0, first + i)),
            pl.BlockSpec((slice_width, head_dim), lambda i: (0, first + i)),
            pl.BlockSpec((slice_width, head_dim), lambda i: (0, first + i)),
        ]

    partials, facts = call(
        project_body,
        [shape((kv_here, steps * rows, width), BF16), shape(facts.shape, F32)],
        (*weights, facts),
        in_specs=weight_specs(0) + [pl.BlockSpec(facts.shape, lambda i: (0, 0))],
        out_specs=[
            pl.BlockSpec((1, steps * rows, width), lambda i: (i, 0, 0)),
            pl.BlockSpec(facts.shape, lambda i: (0, 0)),
        ],
        grid=(kv_here,),
        limit=50,
        flops=2 * steps * rows * slice_width * width * kv_here,
        bytes_=2 * slice_width * width * kv_here,
    )
    share = call(
        functools.partial(shrink_body, home_rows, cap, resident, fold),
        shape((steps * places, 2 * rank), BF16),
        (facts, adapter_down_weight, *sent),
        flops=4 * steps * places * rank * slice_width * fold * resident,
        bytes_=4 * resident * rank * slice_width * fold,
    )
    shares = [share] + [
        lax.ppermute(share, FEATURE_AXES, [(i, i ^ d) for i in range(features)]) for d in range(1, features)
    ]
    cos, sin, length = call(
        functools.partial(home_body, home_rows),
        [shape((local_rows, head_dim), F32)] * 2 + [shape((home_rows, cached), F32)],
        (facts,),
        flops=10**7,
        bytes_=10**5,
    )
    pair = shape((halved, 2 * local_rows, width), BF16)
    message = shape((kv_here - halved, local_rows, width), BF16)

    def expand(heads, paired, after):
        kind = shape((len(heads), (2 if paired else 1) * local_rows, width), BF16)
        return call(
            functools.partial(expand_body, home_rows, homes, heads, paired, features),
            [kind] * (2 if paired else homes),
            (facts, adapter_up_query, adapter_up_value, *shares, partials, *after),
            in_specs=[VMEM] * (4 + features) + [ANY] * len(after),
            scratch=[pltpu.VMEM((steps * rows, width), F32)],
            flops=2 * steps * places * rank * resident * q_cols * len(heads),
            bytes_=2 * resident * rank * q_cols * len(heads),
        )

    direct = tuple(range(halved, kv_here))
    messages = list(expand(direct, False, ()))
    for d in range(2, homes):
        messages[d] = swap(messages[d], d)
    sums = ()
    if halved:
        near, far = expand(tuple(range(halved)), True, messages[:1])
        got = swap(far, 1)
        passed = call(
            add_body,
            shape((halved, local_rows, width), BF16),
            (near, got),
            flops=halved * local_rows * width,
            bytes_=6 * halved * local_rows * width,
        )
        sums = (near, got, swap(passed, 2))
        messages[1] = call(
            pass_body, shape(messages[1].shape, BF16), (messages[1], messages[2]), in_specs=[VMEM, ANY]
        )
    messages[1] = swap(messages[1], 1)

    def attend(heads, pieces, done):
        return call(
            functools.partial(attend_body, home_rows, heads, len(pieces)),
            shape((local_rows, q_cols * (len(heads) + (len(direct) if done else 0))), BF16),
            (cos, sin, length, key_cache_rows, value_cache_rows, *pieces, *done),
            scratch=[pltpu.VMEM((len(heads) * q_cols // head_dim * local_rows, head_dim), F32)] * 4,
            flops=4 * local_rows * q_cols * len(heads) * cached,
            bytes_=4 * home_rows * cached * head_dim * len(heads),
        )

    out = attend(direct, messages, ())
    if halved:
        out = attend(tuple(range(halved)), sums, (out,))
    return out.reshape(steps, home_rows, q_cols * kv_here).transpose(1, 0, 2)


def solution(mesh):
    return jax.shard_map(
        on_device,
        mesh=mesh,
        in_specs=(
            P("groups", None, "pool"),
            P("pool", ("tp", "sub")),
            P("pool", ("tp", "sub")),
            P("pool", ("tp", "sub")),
            P(("groups", "pool"), ("tp", "sub"), None, None),
            P(("groups", "pool"), ("tp", "sub"), None, None),
            P(("groups", "pool"), None, ("tp", "sub")),
            P(("groups", "pool"), None, ("tp", "sub")),
            P(("groups", "pool"), None, ("tp", "sub")),
            P("groups"),
            P("groups"),
            P("groups"),
        ),
        out_specs=P(("groups", "pool"), None, ("tp", "sub")),
        check_vma=False,
    )
```

```python
import functools
import math

import jax
import jax.numpy as jnp
from jax import lax
from jax.experimental import pallas as pl
from jax.experimental.pallas import tpu as pltpu
from jax.sharding import PartitionSpec as P

ROPE_BASE = 500000.0
BF16 = jnp.bfloat16
F32 = jnp.float32
FEATURE_AXES = ("tp", "sub")
CARRIER = ((0, 3, 2, 1), (2, 1, 0, 3), (3, 1, 0, 2), (1, 2, 0, 3))


def call(body, out_shape, args, in_specs=None, out_specs=None, grid=None, scratch=(), flops=0, bytes_=0, limit=40, **more):
    whole = pl.BlockSpec(memory_space=pltpu.VMEM)
    kwargs = {} if grid is None else {"grid": grid}
    if in_specs is None:
        in_specs = [whole] * len(args)
    if out_specs is None:
        out_specs = jax.tree.map(lambda _: whole, out_shape)
    inner = getattr(body, "func", body)
    return pl.pallas_call(
        body,
        name=inner.__name__,
        out_shape=out_shape,
        in_specs=in_specs,
        out_specs=out_specs,
        scratch_shapes=list(scratch),
        compiler_params=pltpu.CompilerParams(vmem_limit_bytes=limit * 1024 * 1024),
        cost_estimate=pl.CostEstimate(flops=flops, bytes_accessed=bytes_, transcendentals=0),
        **kwargs,
        **more,
    )(*args)


VMEM = pl.BlockSpec(memory_space=pltpu.VMEM)
SMEM = pl.BlockSpec(memory_space=pltpu.SMEM)
HBM = pl.BlockSpec(memory_space=pltpu.HBM)
ANY = pl.BlockSpec(memory_space=pl.ANY)


def iota(shape, dim):
    return lax.broadcasted_iota(jnp.int32, shape, dim)


def nn(a, b):
    return lax.dot_general(a, b, (((1,), (0,)), ((), ())), preferred_element_type=F32)


def nt(a, b):
    return lax.dot_general(a, b, (((1,), (1,)), ((), ())), preferred_element_type=F32)


def tn(a, b):
    return lax.dot_general(a, b, (((0,), (0,)), ((), ())), preferred_element_type=F32)


def row_facts(row_request, request_adapter, lengths, home_rows, resident):
    rows = row_request.shape[1]
    across, down = iota((rows, rows), 1), iota((rows, rows), 0)
    eye = across == down
    request_col = jnp.sum(jnp.where(eye, row_request.astype(F32), 0.0), 1, keepdims=True)
    held = request_col == across.astype(F32)
    adapter_col = jnp.sum(jnp.where(held, request_adapter.astype(F32), 0.0), 1, keepdims=True)
    length_col = jnp.sum(jnp.where(held, lengths.astype(F32), 0.0), 1, keepdims=True)
    adapter_row = jnp.sum(jnp.where(eye, adapter_col, 0.0), 0, keepdims=True)
    length_row = jnp.sum(jnp.where(eye, length_col, 0.0), 0, keepdims=True)
    owner_col = jnp.floor((adapter_col + 0.5) / resident)
    owner_row = jnp.floor((adapter_row + 0.5) / resident)
    before = (owner_col == owner_row) & (down < across) & (down // home_rows == across // home_rows)
    slot_row = jnp.sum(jnp.where(before, 1.0, 0.0), 0, keepdims=True)
    return adapter_row, owner_row, slot_row, length_row


def slot_table(owner_row, slot_row, owner, home_rows, cap):
    rows = owner_row.shape[1]
    places = rows // home_rows * cap
    place, row = iota((places, rows), 0), iota((places, rows), 1)
    return (
        (owner_row == owner.astype(F32))
        & (place // cap == row // home_rows)
        & (slot_row == (place % cap).astype(F32))
    )


def select_body(home_rows, cap, resident, owners, rr_hbm, ra_hbm, ln_hbm, hid_hbm, *rest):
    outs, rest = rest[:-6], rest[-6:]
    facts_ref, rr_ref, ra_ref, ln_ref, hid_ref, sems = rest
    copies = [
        pltpu.make_async_copy(source, target, sems.at[n])
        for n, (source, target) in enumerate(
            ((rr_hbm, rr_ref), (ra_hbm, ra_ref), (ln_hbm, ln_ref), (hid_hbm, hid_ref))
        )
    ]
    for copy in copies:
        copy.start()
    for copy in copies[:3]:
        copy.wait()
    adapter_row, owner_row, slot_row, length_row = row_facts(
        rr_ref[...], ra_ref[...], ln_ref[...], home_rows, resident
    )
    facts_ref[...] = jnp.concatenate([adapter_row, owner_row, slot_row, length_row] * 2, 0)
    tables = [
        slot_table(owner_row, slot_row, owner, home_rows, cap).astype(BF16) for owner in owners()
    ]
    copies[3].wait()
    for table, out in zip(tables, outs):
        places = table.shape[0]
        for s in range(hid_ref.shape[0]):
            out[s * places : (s + 1) * places] = nn(table, hid_ref[s]).astype(BF16)


def project_body(x_ref, q_ref, k_ref, v_ref, facts_ref, out, facts_out):
    q_cols = q_ref.shape[1]
    head_dim = k_ref.shape[1]
    facts_out[...] = facts_ref[...]
    out[0, :, :q_cols] = nn(x_ref[...], q_ref[...]).astype(BF16)
    out[0, :, q_cols : q_cols + head_dim] = nn(x_ref[...], k_ref[...]).astype(BF16)
    out[0, :, q_cols + head_dim :] = nn(x_ref[...], v_ref[...]).astype(BF16)


def pass_body(message_ref, _, out_ref):
    out_ref[...] = message_ref[...]


def add_body(near_ref, got_ref, out_ref):
    rows = near_ref.shape[1] // 2
    out_ref[...] = (near_ref[:, rows:].astype(F32) + got_ref[:, rows:].astype(F32)).astype(BF16)


def shrink_body(home_rows, cap, resident, parts, facts_ref, down_ref, *rest):
    sent, out = rest[:parts], rest[-1]
    adapter_row, owner_row, slot_row = facts_ref[0:1], facts_ref[1:2], facts_ref[2:3]
    me = lax.axis_index("pool")
    table = slot_table(owner_row, slot_row, me, home_rows, cap)
    local = jnp.sum(jnp.where(table, adapter_row - (me * resident).astype(F32) + 1.0, 0.0), 1, keepdims=True) - 1.0
    places = table.shape[0]
    steps = sent[0].shape[0] // places
    local = jnp.concatenate([local] * steps, 0)
    width = sent[0].shape[1]
    total = None
    for a in range(resident):
        term = None
        for i in range(parts):
            if parts == 1:
                block = down_ref[a]
            else:
                part = lax.rem(me + parts * places - i, parts)
                block = down_ref[a, :, pl.ds(pl.multiple_of(part * width, width), width)]
            piece = nt(sent[i][...], block)
            term = piece if term is None else term + piece
        term = jnp.where(local == float(a), term, 0.0)
        total = term if total is None else total + term
    out[...] = total.astype(BF16)


def expand_body(home_rows, homes, halved, facts_ref, upq_ref, upv_ref, *rest):
    scr, rest = rest[-1], rest[:-1]
    messages, rest = rest[len(rest) - homes :], rest[: len(rest) - homes]
    if halved:
        (near_ref, far_ref), rest = rest[-2:], rest[:-2]
    shares, partials = rest[:-1], rest[-1]
    adapter_row, owner_row, slot_row = facts_ref[0:1], facts_ref[1:2], facts_ref[2:3]
    me = lax.axis_index("pool")
    resident, rank = upq_ref.shape[:2]
    kv_heads, all_rows, width = partials.shape
    rows = owner_row.shape[1]
    steps = all_rows // rows
    local_rows = steps * home_rows
    shrunk = shares[0][...].astype(F32)
    for share in shares[1:]:
        shrunk = shrunk + share[...].astype(F32)
    places = shrunk.shape[0] // steps
    table = slot_table(owner_row, slot_row, me, home_rows, places // homes)
    local = jnp.sum(jnp.where(table, adapter_row - (me * resident).astype(F32) + 1.0, 0.0), 1, keepdims=True) - 1.0
    spread = table.astype(BF16)
    local = jnp.concatenate([local] * steps, 0)
    low_q, low_v = shrunk[:, :rank], shrunk[:, rank:]
    masked_q = [jnp.where(local == float(a), low_q, 0.0).astype(BF16) for a in range(resident)]
    masked_v = [jnp.where(local == float(a), low_v, 0.0).astype(BF16) for a in range(resident)]
    width_q = upq_ref.shape[2] // kv_heads
    width_v = upv_ref.shape[2] // kv_heads
    for h in range(kv_heads):
        delta_q = delta_v = 0.0
        for a in range(resident):
            delta_q = delta_q + nn(masked_q[a], upq_ref[a, :, h * width_q : (h + 1) * width_q])
            delta_v = delta_v + nn(masked_v[a], upv_ref[a, :, h * width_v : (h + 1) * width_v])
        for s in range(steps):
            here = slice(s * places, (s + 1) * places)
            there = slice(s * rows, (s + 1) * rows)
            middle, end = width_q, width_q + width_v
            scr[there, :middle] = partials[h, there, :middle].astype(F32) + tn(spread, delta_q[here].astype(BF16))
            scr[there, middle:end] = partials[h, there, middle:end].astype(F32)
            scr[there, end:] = partials[h, there, end:].astype(F32) + tn(spread, delta_v[here].astype(BF16))
        for d in range(homes):
            for s in range(steps):
                begin = pl.multiple_of(s * rows + (me ^ d) * home_rows, home_rows)
                row = s * home_rows
                if h < halved:
                    out, at, row = (far_ref if d % 2 else near_ref), h, row + d // 2 * local_rows
                else:
                    out, at = messages[d], h - halved
                out[at, row : row + home_rows, :] = scr[pl.ds(begin, home_rows), :].astype(BF16)


def home_body(home_rows, facts_ref, cos_ref, sin_ref, len_ref):
    length_row = facts_ref[3:4]
    me = lax.axis_index("pool")
    local_rows, head_dim = cos_ref.shape
    rows = facts_ref.shape[1]
    row, batch = iota((local_rows, rows), 0), iota((local_rows, rows), 1)
    mine = batch == me * home_rows + row % home_rows
    length = jnp.sum(jnp.where(mine, length_row, 0.0), 1, keepdims=True)
    len_ref[...] = jnp.broadcast_to(length[:home_rows], len_ref.shape)
    lane = iota((local_rows, head_dim), 1)
    step = iota((local_rows, head_dim), 0) // home_rows
    half = head_dim // 2
    inverse_freq = jnp.exp((lane % half).astype(F32) * (-2.0 * math.log(ROPE_BASE) / head_dim))
    angle = (length + step.astype(F32)) * inverse_freq
    cos_ref[...] = jnp.cos(angle)
    sin_ref[...] = jnp.where(lane < half, -1.0, 1.0) * jnp.sin(angle)


def attend_body(home_rows, which, n_pieces, cos_ref, sin_ref, len_ref, kc_ref, vc_ref, *rest):
    pieces, done, (out, q_scr, new_scr, o_scr, total_scr) = rest[:n_pieces], rest[n_pieces:-5], rest[-5:]
    local_rows, head_dim = cos_ref.shape
    steps = local_rows // home_rows
    cached = kc_ref.shape[2]
    kv_heads = len(which)
    heads = q_scr.shape[0] // (kv_heads * local_rows)
    width_q = heads * head_dim
    scale = 1.0 / math.sqrt(head_dim)
    cos, sin = cos_ref[...], sin_ref[...]

    def rope(v):
        return v * cos + pltpu.roll(v, head_dim // 2, 1) * sin

    def projected(h, begin):
        return sum(piece[h, :local_rows, begin : begin + head_dim].astype(F32) for piece in pieces)

    row, col = iota((local_rows, local_rows), 0), iota((local_rows, local_rows), 1)
    live = (row % home_rows == col % home_rows) & (col // home_rows <= row // home_rows)
    per_row = heads * steps
    spot_ids = iota((per_row, cached), 1).astype(F32)
    every = [(h, b) for h in range(kv_heads) for b in range(home_rows)]
    mine = {
        (h, b): pl.ds(h * heads * local_rows + b, per_row, stride=home_rows) for h, b in every
    }
    new_weights, values_new = {}, {}
    for h in range(kv_heads):
        key_new = rope(projected(h, width_q)).astype(BF16)
        values_new[h] = projected(h, width_q + head_dim).astype(BF16)
        for n in range(heads):
            query = rope(projected(h, n * head_dim)).astype(BF16)
            here = slice((h * heads + n) * local_rows, (h * heads + n + 1) * local_rows)
            q_scr[here, :] = query.astype(F32)
            weight = jnp.where(live, jnp.exp(nt(query, key_new) * scale), 0.0)
            new_weights[h, n] = weight
            new_scr[here, :] = jnp.broadcast_to(jnp.sum(weight, 1, keepdims=True), (local_rows, head_dim))
    for h in range(kv_heads):
        scores = [nt(q_scr[mine[h, b], :].astype(BF16), kc_ref[b, which[h]]) for b in range(home_rows)]
        probs = []
        for b in range(home_rows):
            weight = jnp.where(spot_ids < len_ref[b : b + 1, :], jnp.exp(scores[b] * scale), 0.0)
            total = jnp.sum(weight, 1, keepdims=True) + new_scr[mine[h, b], :][:, :1]
            total_scr[mine[h, b], :] = jnp.broadcast_to(total, (per_row, head_dim))
            probs.append((weight / total).astype(BF16))
        for b in range(home_rows):
            o_scr[mine[h, b], :] = nn(probs[b], vc_ref[b, which[h]])
    for h in range(kv_heads):
        for n in range(heads):
            at = h * heads + n
            here = slice(at * local_rows, (at + 1) * local_rows)
            prob = (new_weights[h, n] / total_scr[here, :local_rows]).astype(BF16)
            out[:, at * head_dim : (at + 1) * head_dim] = (
                o_scr[here, :] + nn(prob, values_new[h])
            ).astype(BF16)
    for piece in done:
        out[:, kv_heads * width_q :] = piece[...]


def on_device(
    hidden,
    query_weight,
    key_weight,
    value_weight,
    key_cache_rows,
    value_cache_rows,
    adapter_down_weight,
    adapter_up_query,
    adapter_up_value,
    request_adapter,
    row_request,
    lengths,
):
    homes = lax.axis_size("pool")
    features = lax.axis_size(FEATURE_AXES)
    home_rows, kv_here, cached, head_dim = key_cache_rows.shape
    rows, steps, slice_width = hidden.shape
    resident = adapter_down_weight.shape[0]
    rank = adapter_up_query.shape[1]
    q_cols = query_weight.shape[1] // kv_here
    cap = max(2, 2 * home_rows // homes)
    places = homes * cap
    fold = homes // features
    local_rows = steps * home_rows
    width = q_cols + 2 * head_dim
    shape = jax.ShapeDtypeStruct

    if homes == len(CARRIER) and features == len(CARRIER):
        targets = [[CARRIER[q].index(g) for g in range(features)] for q in range(homes)]
        perms = [[(q * features + g, targets[q][g] * features + q) for q in range(homes) for g in range(features)]]

        def owners():
            pool_here, feature_here = lax.axis_index("pool"), lax.axis_index(FEATURE_AXES)
            at = pool_here * features + feature_here
            owner = jnp.int32(0)
            for q in range(homes):
                for g in range(features):
                    owner = jnp.where(at == q * features + g, targets[q][g], owner)
            return [owner]

    else:
        perms = [
            [
                (q * features + g, (g * fold + (i + q) % fold) * features + q // fold)
                for q in range(homes)
                for g in range(features)
            ]
            for i in range(fold)
        ]

        def owners():
            pool_here, feature_here = lax.axis_index("pool"), lax.axis_index(FEATURE_AXES)
            return [feature_here * fold + lax.rem(pool_here + i, fold) for i in range(fold)]

    rr, ra, ln = row_request.reshape(1, rows), request_adapter.reshape(1, rows), lengths.reshape(1, rows)
    by_step = hidden.transpose(1, 0, 2)
    x = by_step.reshape(steps * rows, slice_width)
    halved = kv_here // 2 if homes == 4 else 0

    *selected, facts = call(
        functools.partial(select_body, home_rows, cap, resident, owners),
        [shape((steps * places, slice_width), BF16)] * fold + [shape((8, rows), F32)],
        (rr, ra, ln, by_step),
        in_specs=[HBM] * 4,
        limit=60,
        scratch=[pltpu.VMEM((1, rows), jnp.int32)] * 3
        + [pltpu.VMEM(by_step.shape, BF16), pltpu.SemaphoreType.DMA((4,))],
        flops=2 * steps * places * rows * slice_width,
        bytes_=2 * steps * (rows + places) * slice_width,
    )
    sent = [lax.ppermute(s, ("pool", *FEATURE_AXES), perm) for s, perm in zip(selected, perms)]

    def swap(value, d):
        return lax.ppermute(value, "pool", [(i, i ^ d) for i in range(homes)])

    weights = (x, query_weight, key_weight, value_weight)

    def weight_specs(first):
        return [
            pl.BlockSpec(x.shape, lambda i: (0, 0)),
            pl.BlockSpec((slice_width, q_cols), lambda i: (0, first + i)),
            pl.BlockSpec((slice_width, head_dim), lambda i: (0, first + i)),
            pl.BlockSpec((slice_width, head_dim), lambda i: (0, first + i)),
        ]

    partials, facts = call(
        project_body,
        [shape((kv_here, steps * rows, width), BF16), shape(facts.shape, F32)],
        (*weights, facts),
        in_specs=weight_specs(0) + [pl.BlockSpec(facts.shape, lambda i: (0, 0))],
        out_specs=[
            pl.BlockSpec((1, steps * rows, width), lambda i: (i, 0, 0)),
            pl.BlockSpec(facts.shape, lambda i: (0, 0)),
        ],
        grid=(kv_here,),
        limit=50,
        flops=2 * steps * rows * slice_width * width * kv_here,
        bytes_=2 * slice_width * width * kv_here,
    )
    share = call(
        functools.partial(shrink_body, home_rows, cap, resident, fold),
        shape((steps * places, 2 * rank), BF16),
        (facts, adapter_down_weight, *sent),
        flops=4 * steps * places * rank * slice_width * fold * resident,
        bytes_=4 * resident * rank * slice_width * fold,
    )
    shares = [share] + [
        lax.ppermute(share, FEATURE_AXES, [(i, i ^ d) for i in range(features)]) for d in range(1, features)
    ]
    cos, sin, length = call(
        functools.partial(home_body, home_rows),
        [shape((local_rows, head_dim), F32)] * 2 + [shape((home_rows, cached), F32)],
        (facts,),
        flops=10**7,
        bytes_=10**5,
    )
    pair = shape((halved, 2 * local_rows, width), BF16)
    message = shape((kv_here - halved, local_rows, width), BF16)

    direct = tuple(range(halved, kv_here))
    pair = shape((halved, 2 * local_rows, width), BF16)
    grown = call(
        functools.partial(expand_body, home_rows, homes, halved),
        [pair] * (2 if halved else 0) + [shape((len(direct), local_rows, width), BF16)] * homes,
        (facts, adapter_up_query, adapter_up_value, *shares, partials),
        scratch=[pltpu.VMEM((steps * rows, width), F32)],
        flops=2 * steps * places * rank * resident * q_cols * kv_here,
        bytes_=2 * resident * rank * q_cols * kv_here,
    )
    messages = list(grown[-homes:])
    for d in range(2, homes):
        messages[d] = swap(messages[d], d)
    sums = ()
    if halved:
        near, far = grown[:2]
        got = swap(far, 1)
        passed = call(
            add_body,
            shape((halved, local_rows, width), BF16),
            (near, got),
            flops=halved * local_rows * width,
            bytes_=6 * halved * local_rows * width,
        )
        sums = (near, got, swap(passed, 2))
        messages[1] = call(
            pass_body, shape(messages[1].shape, BF16), (messages[1], messages[2]), in_specs=[VMEM, ANY]
        )
    messages[1] = swap(messages[1], 1)

    def attend(heads, pieces, done):
        return call(
            functools.partial(attend_body, home_rows, heads, len(pieces)),
            shape((local_rows, q_cols * (len(heads) + (len(direct) if done else 0))), BF16),
            (cos, sin, length, key_cache_rows, value_cache_rows, *pieces, *done),
            scratch=[pltpu.VMEM((len(heads) * q_cols // head_dim * local_rows, head_dim), F32)] * 4,
            flops=4 * local_rows * q_cols * len(heads) * cached,
            bytes_=4 * home_rows * cached * head_dim * len(heads),
        )

    out = attend(direct, messages, ())
    if halved:
        out = attend(tuple(range(halved)), sums, (out,))
    return out.reshape(steps, home_rows, q_cols * kv_here).transpose(1, 0, 2)


def solution(mesh):
    return jax.shard_map(
        on_device,
        mesh=mesh,
        in_specs=(
            P("groups", None, "pool"),
            P("pool", ("tp", "sub")),
            P("pool", ("tp", "sub")),
            P("pool", ("tp", "sub")),
            P(("groups", "pool"), ("tp", "sub"), None, None),
            P(("groups", "pool"), ("tp", "sub"), None, None),
            P(("groups", "pool"), None, ("tp", "sub")),
            P(("groups", "pool"), None, ("tp", "sub")),
            P(("groups", "pool"), None, ("tp", "sub")),
            P("groups"),
            P("groups"),
            P("groups"),
        ),
        out_specs=P(("groups", "pool"), None, ("tp", "sub")),
        check_vma=False,
    )
```

```python
import functools
import math

import jax
import jax.numpy as jnp
from jax import lax
from jax.experimental import pallas as pl
from jax.experimental.pallas import tpu as pltpu
from jax.sharding import PartitionSpec as P

ROPE_BASE = 500000.0
BF16 = jnp.bfloat16
F32 = jnp.float32
FEATURE_AXES = ("tp", "sub")
CARRIER = ((3, 1, 2, 0), (1, 2, 3, 0), (3, 1, 0, 2), (1, 3, 2, 0))


def call(body, out_shape, args, in_specs=None, out_specs=None, grid=None, scratch=(), flops=0, bytes_=0, limit=40, **more):
    whole = pl.BlockSpec(memory_space=pltpu.VMEM)
    kwargs = {} if grid is None else {"grid": grid}
    if in_specs is None:
        in_specs = [whole] * len(args)
    if out_specs is None:
        out_specs = jax.tree.map(lambda _: whole, out_shape)
    inner = getattr(body, "func", body)
    return pl.pallas_call(
        body,
        name=inner.__name__,
        out_shape=out_shape,
        in_specs=in_specs,
        out_specs=out_specs,
        scratch_shapes=list(scratch),
        compiler_params=pltpu.CompilerParams(vmem_limit_bytes=limit * 1024 * 1024),
        cost_estimate=pl.CostEstimate(flops=flops, bytes_accessed=bytes_, transcendentals=0),
        **kwargs,
        **more,
    )(*args)


VMEM = pl.BlockSpec(memory_space=pltpu.VMEM)
SMEM = pl.BlockSpec(memory_space=pltpu.SMEM)
HBM = pl.BlockSpec(memory_space=pltpu.HBM)
ANY = pl.BlockSpec(memory_space=pl.ANY)


def iota(shape, dim):
    return lax.broadcasted_iota(jnp.int32, shape, dim)


def nn(a, b):
    return lax.dot_general(a, b, (((1,), (0,)), ((), ())), preferred_element_type=F32)


def nt(a, b):
    return lax.dot_general(a, b, (((1,), (1,)), ((), ())), preferred_element_type=F32)


def tn(a, b):
    return lax.dot_general(a, b, (((0,), (0,)), ((), ())), preferred_element_type=F32)


def row_facts(row_request, request_adapter, lengths, home_rows, resident):
    rows = row_request.shape[1]
    across, down = iota((rows, rows), 1), iota((rows, rows), 0)
    eye = across == down
    request_col = jnp.sum(jnp.where(eye, row_request.astype(F32), 0.0), 1, keepdims=True)
    held = request_col == across.astype(F32)
    adapter_col = jnp.sum(jnp.where(held, request_adapter.astype(F32), 0.0), 1, keepdims=True)
    length_col = jnp.sum(jnp.where(held, lengths.astype(F32), 0.0), 1, keepdims=True)
    adapter_row = jnp.sum(jnp.where(eye, adapter_col, 0.0), 0, keepdims=True)
    length_row = jnp.sum(jnp.where(eye, length_col, 0.0), 0, keepdims=True)
    owner_col = jnp.floor((adapter_col + 0.5) / resident)
    owner_row = jnp.floor((adapter_row + 0.5) / resident)
    before = (owner_col == owner_row) & (down < across) & (down // home_rows == across // home_rows)
    slot_row = jnp.sum(jnp.where(before, 1.0, 0.0), 0, keepdims=True)
    return adapter_row, owner_row, slot_row, length_row


def slot_table(owner_row, slot_row, owner, home_rows, cap):
    rows = owner_row.shape[1]
    places = rows // home_rows * cap
    place, row = iota((places, rows), 0), iota((places, rows), 1)
    return (
        (owner_row == owner.astype(F32))
        & (place // cap == row // home_rows)
        & (slot_row == (place % cap).astype(F32))
    )


def select_body(home_rows, cap, resident, owners, rr_hbm, ra_hbm, ln_hbm, hid_hbm, *rest):
    outs, rest = rest[:-6], rest[-6:]
    facts_ref, rr_ref, ra_ref, ln_ref, hid_ref, sems = rest
    copies = [
        pltpu.make_async_copy(source, target, sems.at[n])
        for n, (source, target) in enumerate(
            ((rr_hbm, rr_ref), (ra_hbm, ra_ref), (ln_hbm, ln_ref), (hid_hbm, hid_ref))
        )
    ]
    for copy in copies:
        copy.start()
    for copy in copies[:3]:
        copy.wait()
    adapter_row, owner_row, slot_row, length_row = row_facts(
        rr_ref[...], ra_ref[...], ln_ref[...], home_rows, resident
    )
    facts_ref[...] = jnp.concatenate([adapter_row, owner_row, slot_row, length_row] * 2, 0)
    tables = [
        slot_table(owner_row, slot_row, owner, home_rows, cap).astype(BF16) for owner in owners()
    ]
    copies[3].wait()
    for table, out in zip(tables, outs):
        places = table.shape[0]
        for s in range(hid_ref.shape[0]):
            out[s * places : (s + 1) * places] = nn(table, hid_ref[s]).astype(BF16)


def project_body(x_ref, q_ref, k_ref, v_ref, facts_ref, out, facts_out):
    q_cols = q_ref.shape[1]
    head_dim = k_ref.shape[1]
    facts_out[...] = facts_ref[...]
    out[0, :, :q_cols] = nn(x_ref[...], q_ref[...]).astype(BF16)
    out[0, :, q_cols : q_cols + head_dim] = nn(x_ref[...], k_ref[...]).astype(BF16)
    out[0, :, q_cols + head_dim :] = nn(x_ref[...], v_ref[...]).astype(BF16)


def pass_body(message_ref, _, out_ref):
    out_ref[...] = message_ref[...]


def add_body(near_ref, got_ref, out_ref):
    rows = near_ref.shape[1] // 2
    out_ref[...] = (near_ref[:, rows:].astype(F32) + got_ref[:, rows:].astype(F32)).astype(BF16)


def shrink_body(home_rows, cap, resident, parts, facts_ref, down_ref, *rest):
    sent, out = rest[:parts], rest[-1]
    adapter_row, owner_row, slot_row = facts_ref[0:1], facts_ref[1:2], facts_ref[2:3]
    me = lax.axis_index("pool")
    table = slot_table(owner_row, slot_row, me, home_rows, cap)
    local = jnp.sum(jnp.where(table, adapter_row - (me * resident).astype(F32) + 1.0, 0.0), 1, keepdims=True) - 1.0
    places = table.shape[0]
    steps = sent[0].shape[0] // places
    local = jnp.concatenate([local] * steps, 0)
    width = sent[0].shape[1]
    total = None
    for a in range(resident):
        term = None
        for i in range(parts):
            if parts == 1:
                block = down_ref[a]
            else:
                part = lax.rem(me + parts * places - i, parts)
                block = down_ref[a, :, pl.ds(pl.multiple_of(part * width, width), width)]
            piece = nt(sent[i][...], block)
            term = piece if term is None else term + piece
        term = jnp.where(local == float(a), term, 0.0)
        total = term if total is None else total + term
    out[...] = total.astype(BF16)


def expand_body(home_rows, homes, halved, facts_ref, upq_ref, upv_ref, *rest):
    scr, rest = rest[-1], rest[:-1]
    messages, rest = rest[len(rest) - homes :], rest[: len(rest) - homes]
    if halved:
        (near_ref, far_ref), rest = rest[-2:], rest[:-2]
    shares, partials = rest[:-1], rest[-1]
    adapter_row, owner_row, slot_row = facts_ref[0:1], facts_ref[1:2], facts_ref[2:3]
    me = lax.axis_index("pool")
    resident, rank = upq_ref.shape[:2]
    kv_heads, all_rows, width = partials.shape
    rows = owner_row.shape[1]
    steps = all_rows // rows
    local_rows = steps * home_rows
    shrunk = shares[0][...].astype(F32)
    for share in shares[1:]:
        shrunk = shrunk + share[...].astype(F32)
    places = shrunk.shape[0] // steps
    table = slot_table(owner_row, slot_row, me, home_rows, places // homes)
    local = jnp.sum(jnp.where(table, adapter_row - (me * resident).astype(F32) + 1.0, 0.0), 1, keepdims=True) - 1.0
    spread = table.astype(BF16)
    local = jnp.concatenate([local] * steps, 0)
    low_q, low_v = shrunk[:, :rank], shrunk[:, rank:]
    masked_q = [jnp.where(local == float(a), low_q, 0.0).astype(BF16) for a in range(resident)]
    masked_v = [jnp.where(local == float(a), low_v, 0.0).astype(BF16) for a in range(resident)]
    width_q = upq_ref.shape[2] // kv_heads
    width_v = upv_ref.shape[2] // kv_heads
    for h in range(kv_heads):
        delta_q = delta_v = 0.0
        for a in range(resident):
            delta_q = delta_q + nn(masked_q[a], upq_ref[a, :, h * width_q : (h + 1) * width_q])
            delta_v = delta_v + nn(masked_v[a], upv_ref[a, :, h * width_v : (h + 1) * width_v])
        for s in range(steps):
            here = slice(s * places, (s + 1) * places)
            there = slice(s * rows, (s + 1) * rows)
            middle, end = width_q, width_q + width_v
            scr[there, :middle] = partials[h, there, :middle].astype(F32) + tn(spread, delta_q[here].astype(BF16))
            scr[there, middle:end] = partials[h, there, middle:end].astype(F32)
            scr[there, end:] = partials[h, there, end:].astype(F32) + tn(spread, delta_v[here].astype(BF16))
        for d in range(homes):
            for s in range(steps):
                begin = pl.multiple_of(s * rows + (me ^ d) * home_rows, home_rows)
                row = s * home_rows
                if h < halved:
                    out, at, row = (far_ref if d % 2 else near_ref), h, row + d // 2 * local_rows
                else:
                    out, at = messages[d], h - halved
                out[at, row : row + home_rows, :] = scr[pl.ds(begin, home_rows), :].astype(BF16)


def home_body(home_rows, facts_ref, cos_ref, sin_ref, len_ref):
    length_row = facts_ref[3:4]
    me = lax.axis_index("pool")
    local_rows, head_dim = cos_ref.shape
    rows = facts_ref.shape[1]
    row, batch = iota((local_rows, rows), 0), iota((local_rows, rows), 1)
    mine = batch == me * home_rows + row % home_rows
    length = jnp.sum(jnp.where(mine, length_row, 0.0), 1, keepdims=True)
    len_ref[...] = jnp.broadcast_to(length[:home_rows], len_ref.shape)
    lane = iota((local_rows, head_dim), 1)
    step = iota((local_rows, head_dim), 0) // home_rows
    half = head_dim // 2
    inverse_freq = jnp.exp((lane % half).astype(F32) * (-2.0 * math.log(ROPE_BASE) / head_dim))
    angle = (length + step.astype(F32)) * inverse_freq
    cos_ref[...] = jnp.cos(angle)
    sin_ref[...] = jnp.where(lane < half, -1.0, 1.0) * jnp.sin(angle)


def attend_body(home_rows, which, n_pieces, cos_ref, sin_ref, len_ref, kc_ref, vc_ref, *rest):
    pieces, done, (out, q_scr, new_scr, o_scr, total_scr) = rest[:n_pieces], rest[n_pieces:-5], rest[-5:]
    local_rows, head_dim = cos_ref.shape
    steps = local_rows // home_rows
    cached = kc_ref.shape[2]
    kv_heads = len(which)
    heads = q_scr.shape[0] // (kv_heads * local_rows)
    width_q = heads * head_dim
    scale = 1.0 / math.sqrt(head_dim)
    cos, sin = cos_ref[...], sin_ref[...]

    def rope(v):
        return v * cos + pltpu.roll(v, head_dim // 2, 1) * sin

    def projected(h, begin):
        return sum(piece[h, :local_rows, begin : begin + head_dim].astype(F32) for piece in pieces)

    row, col = iota((local_rows, local_rows), 0), iota((local_rows, local_rows), 1)
    live = (row % home_rows == col % home_rows) & (col // home_rows <= row // home_rows)
    per_row = heads * steps
    spot_ids = iota((per_row, cached), 1).astype(F32)
    every = [(h, b) for h in range(kv_heads) for b in range(home_rows)]
    mine = {
        (h, b): pl.ds(h * heads * local_rows + b, per_row, stride=home_rows) for h, b in every
    }
    new_weights, values_new = {}, {}
    for h in range(kv_heads):
        key_new = rope(projected(h, width_q)).astype(BF16)
        values_new[h] = projected(h, width_q + head_dim).astype(BF16)
        for n in range(heads):
            query = rope(projected(h, n * head_dim)).astype(BF16)
            here = slice((h * heads + n) * local_rows, (h * heads + n + 1) * local_rows)
            q_scr[here, :] = query.astype(F32)
            weight = jnp.where(live, jnp.exp(nt(query, key_new) * scale), 0.0)
            new_weights[h, n] = weight
            new_scr[here, :] = jnp.broadcast_to(jnp.sum(weight, 1, keepdims=True), (local_rows, head_dim))
    for h in range(kv_heads):
        scores = [nt(q_scr[mine[h, b], :].astype(BF16), kc_ref[b, which[h]]) for b in range(home_rows)]
        probs = []
        for b in range(home_rows):
            weight = jnp.where(spot_ids < len_ref[b : b + 1, :], jnp.exp(scores[b] * scale), 0.0)
            total = jnp.sum(weight, 1, keepdims=True) + new_scr[mine[h, b], :][:, :1]
            total_scr[mine[h, b], :] = jnp.broadcast_to(total, (per_row, head_dim))
            probs.append((weight / total).astype(BF16))
        for b in range(home_rows):
            o_scr[mine[h, b], :] = nn(probs[b], vc_ref[b, which[h]])
    for h in range(kv_heads):
        for n in range(heads):
            at = h * heads + n
            here = slice(at * local_rows, (at + 1) * local_rows)
            prob = (new_weights[h, n] / total_scr[here, :local_rows]).astype(BF16)
            out[:, at * head_dim : (at + 1) * head_dim] = (
                o_scr[here, :] + nn(prob, values_new[h])
            ).astype(BF16)
    for piece in done:
        out[:, kv_heads * width_q :] = piece[...]


def on_device(
    hidden,
    query_weight,
    key_weight,
    value_weight,
    key_cache_rows,
    value_cache_rows,
    adapter_down_weight,
    adapter_up_query,
    adapter_up_value,
    request_adapter,
    row_request,
    lengths,
):
    homes = lax.axis_size("pool")
    features = lax.axis_size(FEATURE_AXES)
    home_rows, kv_here, cached, head_dim = key_cache_rows.shape
    rows, steps, slice_width = hidden.shape
    resident = adapter_down_weight.shape[0]
    rank = adapter_up_query.shape[1]
    q_cols = query_weight.shape[1] // kv_here
    cap = max(2, 2 * home_rows // homes)
    places = homes * cap
    fold = homes // features
    local_rows = steps * home_rows
    width = q_cols + 2 * head_dim
    shape = jax.ShapeDtypeStruct

    if homes == len(CARRIER) and features == len(CARRIER):
        targets = [[CARRIER[q].index(g) for g in range(features)] for q in range(homes)]
        perms = [[(q * features + g, targets[q][g] * features + q) for q in range(homes) for g in range(features)]]

        def owners():
            pool_here, feature_here = lax.axis_index("pool"), lax.axis_index(FEATURE_AXES)
            at = pool_here * features + feature_here
            owner = jnp.int32(0)
            for q in range(homes):
                for g in range(features):
                    owner = jnp.where(at == q * features + g, targets[q][g], owner)
            return [owner]

    else:
        perms = [
            [
                (q * features + g, (g * fold + (i + q) % fold) * features + q // fold)
                for q in range(homes)
                for g in range(features)
            ]
            for i in range(fold)
        ]

        def owners():
            pool_here, feature_here = lax.axis_index("pool"), lax.axis_index(FEATURE_AXES)
            return [feature_here * fold + lax.rem(pool_here + i, fold) for i in range(fold)]

    rr, ra, ln = row_request.reshape(1, rows), request_adapter.reshape(1, rows), lengths.reshape(1, rows)
    by_step = hidden.transpose(1, 0, 2)
    x = by_step.reshape(steps * rows, slice_width)
    halved = kv_here // 2 if homes == 4 else 0

    *selected, facts = call(
        functools.partial(select_body, home_rows, cap, resident, owners),
        [shape((steps * places, slice_width), BF16)] * fold + [shape((8, rows), F32)],
        (rr, ra, ln, by_step),
        in_specs=[HBM] * 4,
        limit=60,
        scratch=[pltpu.VMEM((1, rows), jnp.int32)] * 3
        + [pltpu.VMEM(by_step.shape, BF16), pltpu.SemaphoreType.DMA((4,))],
        flops=2 * steps * places * rows * slice_width,
        bytes_=2 * steps * (rows + places) * slice_width,
    )
    sent = [lax.ppermute(s, ("pool", *FEATURE_AXES), perm) for s, perm in zip(selected, perms)]

    def swap(value, d):
        return lax.ppermute(value, "pool", [(i, i ^ d) for i in range(homes)])

    weights = (x, query_weight, key_weight, value_weight)

    def weight_specs(first):
        return [
            pl.BlockSpec(x.shape, lambda i: (0, 0)),
            pl.BlockSpec((slice_width, q_cols), lambda i: (0, first + i)),
            pl.BlockSpec((slice_width, head_dim), lambda i: (0, first + i)),
            pl.BlockSpec((slice_width, head_dim), lambda i: (0, first + i)),
        ]

    partials, facts = call(
        project_body,
        [shape((kv_here, steps * rows, width), BF16), shape(facts.shape, F32)],
        (*weights, facts),
        in_specs=weight_specs(0) + [pl.BlockSpec(facts.shape, lambda i: (0, 0))],
        out_specs=[
            pl.BlockSpec((1, steps * rows, width), lambda i: (i, 0, 0)),
            pl.BlockSpec(facts.shape, lambda i: (0, 0)),
        ],
        grid=(kv_here,),
        limit=50,
        flops=2 * steps * rows * slice_width * width * kv_here,
        bytes_=2 * slice_width * width * kv_here,
    )
    share = call(
        functools.partial(shrink_body, home_rows, cap, resident, fold),
        shape((steps * places, 2 * rank), BF16),
        (facts, adapter_down_weight, *sent),
        flops=4 * steps * places * rank * slice_width * fold * resident,
        bytes_=4 * resident * rank * slice_width * fold,
    )
    shares = [share] + [
        lax.ppermute(share, FEATURE_AXES, [(i, i ^ d) for i in range(features)]) for d in range(1, features)
    ]
    cos, sin, length = call(
        functools.partial(home_body, home_rows),
        [shape((local_rows, head_dim), F32)] * 2 + [shape((home_rows, cached), F32)],
        (facts,),
        flops=10**7,
        bytes_=10**5,
    )
    pair = shape((halved, 2 * local_rows, width), BF16)
    message = shape((kv_here - halved, local_rows, width), BF16)

    direct = tuple(range(halved, kv_here))
    pair = shape((halved, 2 * local_rows, width), BF16)
    grown = call(
        functools.partial(expand_body, home_rows, homes, halved),
        [pair] * (2 if halved else 0) + [shape((len(direct), local_rows, width), BF16)] * homes,
        (facts, adapter_up_query, adapter_up_value, *shares, partials),
        scratch=[pltpu.VMEM((steps * rows, width), F32)],
        flops=2 * steps * places * rank * resident * q_cols * kv_here,
        bytes_=2 * resident * rank * q_cols * kv_here,
    )
    messages = list(grown[-homes:])
    for d in range(2, homes):
        messages[d] = swap(messages[d], d)
    sums = ()
    if halved:
        near, far = grown[:2]
        got = swap(far, 1)
        passed = call(
            add_body,
            shape((halved, local_rows, width), BF16),
            (near, got),
            flops=halved * local_rows * width,
            bytes_=6 * halved * local_rows * width,
        )
        sums = (near, got, swap(passed, 2))
        messages[1] = call(
            pass_body, shape(messages[1].shape, BF16), (messages[1], passed), in_specs=[VMEM, ANY]
        )
    messages[1] = swap(messages[1], 1)

    def attend(heads, pieces, done):
        return call(
            functools.partial(attend_body, home_rows, heads, len(pieces)),
            shape((local_rows, q_cols * (len(heads) + (len(direct) if done else 0))), BF16),
            (cos, sin, length, key_cache_rows, value_cache_rows, *pieces, *done),
            scratch=[pltpu.VMEM((len(heads) * q_cols // head_dim * local_rows, head_dim), F32)] * 4,
            flops=4 * local_rows * q_cols * len(heads) * cached,
            bytes_=4 * home_rows * cached * head_dim * len(heads),
        )

    out = attend(direct, messages, ())
    if halved:
        out = attend(tuple(range(halved)), sums, (out,))
    return out.reshape(steps, home_rows, q_cols * kv_here).transpose(1, 0, 2)


def solution(mesh):
    return jax.shard_map(
        on_device,
        mesh=mesh,
        in_specs=(
            P("groups", None, "pool"),
            P("pool", ("tp", "sub")),
            P("pool", ("tp", "sub")),
            P("pool", ("tp", "sub")),
            P(("groups", "pool"), ("tp", "sub"), None, None),
            P(("groups", "pool"), ("tp", "sub"), None, None),
            P(("groups", "pool"), None, ("tp", "sub")),
            P(("groups", "pool"), None, ("tp", "sub")),
            P(("groups", "pool"), None, ("tp", "sub")),
            P("groups"),
            P("groups"),
            P("groups"),
        ),
        out_specs=P(("groups", "pool"), None, ("tp", "sub")),
        check_vma=False,
    )
```

```python
import functools
import math

import jax
import jax.numpy as jnp
from jax import lax
from jax.experimental import pallas as pl
from jax.experimental.pallas import tpu as pltpu
from jax.sharding import PartitionSpec as P

ROPE_BASE = 500000.0
BF16 = jnp.bfloat16
F32 = jnp.float32
FEATURE_AXES = ("tp", "sub")
CARRIER = ((3, 1, 2, 0), (1, 2, 3, 0), (3, 1, 0, 2), (1, 3, 2, 0))


def call(body, out_shape, args, in_specs=None, out_specs=None, grid=None, scratch=(), flops=0, bytes_=0, limit=40, **more):
    whole = pl.BlockSpec(memory_space=pltpu.VMEM)
    kwargs = {} if grid is None else {"grid": grid}
    if in_specs is None:
        in_specs = [whole] * len(args)
    if out_specs is None:
        out_specs = jax.tree.map(lambda _: whole, out_shape)
    inner = getattr(body, "func", body)
    return pl.pallas_call(
        body,
        name=inner.__name__,
        out_shape=out_shape,
        in_specs=in_specs,
        out_specs=out_specs,
        scratch_shapes=list(scratch),
        compiler_params=pltpu.CompilerParams(vmem_limit_bytes=limit * 1024 * 1024),
        cost_estimate=pl.CostEstimate(flops=flops, bytes_accessed=bytes_, transcendentals=0),
        **kwargs,
        **more,
    )(*args)


VMEM = pl.BlockSpec(memory_space=pltpu.VMEM)
SMEM = pl.BlockSpec(memory_space=pltpu.SMEM)
HBM = pl.BlockSpec(memory_space=pltpu.HBM)
ANY = pl.BlockSpec(memory_space=pl.ANY)


def iota(shape, dim):
    return lax.broadcasted_iota(jnp.int32, shape, dim)


def nn(a, b):
    return lax.dot_general(a, b, (((1,), (0,)), ((), ())), preferred_element_type=F32)


def nt(a, b):
    return lax.dot_general(a, b, (((1,), (1,)), ((), ())), preferred_element_type=F32)


def tn(a, b):
    return lax.dot_general(a, b, (((0,), (0,)), ((), ())), preferred_element_type=F32)


def row_facts(row_request, request_adapter, lengths, home_rows, resident):
    rows = row_request.shape[1]
    across, down = iota((rows, rows), 1), iota((rows, rows), 0)
    eye = across == down
    request_col = jnp.sum(jnp.where(eye, row_request.astype(F32), 0.0), 1, keepdims=True)
    held = request_col == across.astype(F32)
    adapter_col = jnp.sum(jnp.where(held, request_adapter.astype(F32), 0.0), 1, keepdims=True)
    length_col = jnp.sum(jnp.where(held, lengths.astype(F32), 0.0), 1, keepdims=True)
    adapter_row = jnp.sum(jnp.where(eye, adapter_col, 0.0), 0, keepdims=True)
    length_row = jnp.sum(jnp.where(eye, length_col, 0.0), 0, keepdims=True)
    owner_col = jnp.floor((adapter_col + 0.5) / resident)
    owner_row = jnp.floor((adapter_row + 0.5) / resident)
    before = (owner_col == owner_row) & (down < across) & (down // home_rows == across // home_rows)
    slot_row = jnp.sum(jnp.where(before, 1.0, 0.0), 0, keepdims=True)
    return adapter_row, owner_row, slot_row, length_row


def slot_table(owner_row, slot_row, owner, home_rows, cap):
    rows = owner_row.shape[1]
    places = rows // home_rows * cap
    place, row = iota((places, rows), 0), iota((places, rows), 1)
    return (
        (owner_row == owner.astype(F32))
        & (place // cap == row // home_rows)
        & (slot_row == (place % cap).astype(F32))
    )


def select_body(home_rows, cap, resident, owners, rr_hbm, ra_hbm, ln_hbm, hid_hbm, *rest):
    outs, rest = rest[:-6], rest[-6:]
    facts_ref, rr_ref, ra_ref, ln_ref, hid_ref, sems = rest
    copies = [
        pltpu.make_async_copy(source, target, sems.at[n])
        for n, (source, target) in enumerate(
            ((rr_hbm, rr_ref), (ra_hbm, ra_ref), (ln_hbm, ln_ref), (hid_hbm, hid_ref))
        )
    ]
    for copy in copies:
        copy.start()
    for copy in copies[:3]:
        copy.wait()
    adapter_row, owner_row, slot_row, length_row = row_facts(
        rr_ref[...], ra_ref[...], ln_ref[...], home_rows, resident
    )
    facts_ref[...] = jnp.concatenate([adapter_row, owner_row, slot_row, length_row] * 2, 0)
    tables = [
        slot_table(owner_row, slot_row, owner, home_rows, cap).astype(BF16) for owner in owners()
    ]
    copies[3].wait()
    for table, out in zip(tables, outs):
        places = table.shape[0]
        for s in range(hid_ref.shape[0]):
            out[s * places : (s + 1) * places] = nn(table, hid_ref[s]).astype(BF16)


def project_body(x_ref, q_ref, k_ref, v_ref, facts_ref, out, facts_out):
    q_cols = q_ref.shape[1]
    head_dim = k_ref.shape[1]
    facts_out[...] = facts_ref[...]
    out[0, :, :q_cols] = nn(x_ref[...], q_ref[...]).astype(BF16)
    out[0, :, q_cols : q_cols + head_dim] = nn(x_ref[...], k_ref[...]).astype(BF16)
    out[0, :, q_cols + head_dim :] = nn(x_ref[...], v_ref[...]).astype(BF16)


def add_body(near_ref, got_ref, message_ref, out_ref, message_out):
    rows = near_ref.shape[1] // 2
    out_ref[...] = (near_ref[:, rows:].astype(F32) + got_ref[:, rows:].astype(F32)).astype(BF16)
    message_out[...] = message_ref[...]


def shrink_body(home_rows, cap, resident, parts, facts_ref, down_ref, *rest):
    sent, out = rest[:parts], rest[-1]
    adapter_row, owner_row, slot_row = facts_ref[0:1], facts_ref[1:2], facts_ref[2:3]
    me = lax.axis_index("pool")
    table = slot_table(owner_row, slot_row, me, home_rows, cap)
    local = jnp.sum(jnp.where(table, adapter_row - (me * resident).astype(F32) + 1.0, 0.0), 1, keepdims=True) - 1.0
    places = table.shape[0]
    steps = sent[0].shape[0] // places
    local = jnp.concatenate([local] * steps, 0)
    width = sent[0].shape[1]
    total = None
    for a in range(resident):
        term = None
        for i in range(parts):
            if parts == 1:
                block = down_ref[a]
            else:
                part = lax.rem(me + parts * places - i, parts)
                block = down_ref[a, :, pl.ds(pl.multiple_of(part * width, width), width)]
            piece = nt(sent[i][...], block)
            term = piece if term is None else term + piece
        term = jnp.where(local == float(a), term, 0.0)
        total = term if total is None else total + term
    out[...] = total.astype(BF16)


def expand_body(home_rows, homes, halved, facts_ref, upq_ref, upv_ref, *rest):
    scr, rest = rest[-1], rest[:-1]
    messages, rest = rest[len(rest) - homes :], rest[: len(rest) - homes]
    if halved:
        (near_ref, far_ref), rest = rest[-2:], rest[:-2]
    shares, partials = rest[:-1], rest[-1]
    adapter_row, owner_row, slot_row = facts_ref[0:1], facts_ref[1:2], facts_ref[2:3]
    me = lax.axis_index("pool")
    resident, rank = upq_ref.shape[:2]
    kv_heads, all_rows, width = partials.shape
    rows = owner_row.shape[1]
    steps = all_rows // rows
    local_rows = steps * home_rows
    shrunk = shares[0][...].astype(F32)
    for share in shares[1:]:
        shrunk = shrunk + share[...].astype(F32)
    places = shrunk.shape[0] // steps
    table = slot_table(owner_row, slot_row, me, home_rows, places // homes)
    local = jnp.sum(jnp.where(table, adapter_row - (me * resident).astype(F32) + 1.0, 0.0), 1, keepdims=True) - 1.0
    spread = table.astype(BF16)
    local = jnp.concatenate([local] * steps, 0)
    low_q, low_v = shrunk[:, :rank], shrunk[:, rank:]
    masked_q = [jnp.where(local == float(a), low_q, 0.0).astype(BF16) for a in range(resident)]
    masked_v = [jnp.where(local == float(a), low_v, 0.0).astype(BF16) for a in range(resident)]
    width_q = upq_ref.shape[2] // kv_heads
    width_v = upv_ref.shape[2] // kv_heads
    for h in range(kv_heads):
        delta_q = delta_v = 0.0
        for a in range(resident):
            delta_q = delta_q + nn(masked_q[a], upq_ref[a, :, h * width_q : (h + 1) * width_q])
            delta_v = delta_v + nn(masked_v[a], upv_ref[a, :, h * width_v : (h + 1) * width_v])
        for s in range(steps):
            here = slice(s * places, (s + 1) * places)
            there = slice(s * rows, (s + 1) * rows)
            middle, end = width_q, width_q + width_v
            scr[there, :middle] = partials[h, there, :middle].astype(F32) + tn(spread, delta_q[here].astype(BF16))
            scr[there, middle:end] = partials[h, there, middle:end].astype(F32)
            scr[there, end:] = partials[h, there, end:].astype(F32) + tn(spread, delta_v[here].astype(BF16))
        for d in range(homes):
            for s in range(steps):
                begin = pl.multiple_of(s * rows + (me ^ d) * home_rows, home_rows)
                row = s * home_rows
                if h < halved:
                    out, at, row = (far_ref if d % 2 else near_ref), h, row + d // 2 * local_rows
                else:
                    out, at = messages[d], h - halved
                out[at, row : row + home_rows, :] = scr[pl.ds(begin, home_rows), :].astype(BF16)


def home_body(home_rows, facts_ref, cos_ref, sin_ref, len_ref):
    length_row = facts_ref[3:4]
    me = lax.axis_index("pool")
    local_rows, head_dim = cos_ref.shape
    rows = facts_ref.shape[1]
    row, batch = iota((local_rows, rows), 0), iota((local_rows, rows), 1)
    mine = batch == me * home_rows + row % home_rows
    length = jnp.sum(jnp.where(mine, length_row, 0.0), 1, keepdims=True)
    len_ref[...] = jnp.broadcast_to(length[:home_rows], len_ref.shape)
    lane = iota((local_rows, head_dim), 1)
    step = iota((local_rows, head_dim), 0) // home_rows
    half = head_dim // 2
    inverse_freq = jnp.exp((lane % half).astype(F32) * (-2.0 * math.log(ROPE_BASE) / head_dim))
    angle = (length + step.astype(F32)) * inverse_freq
    cos_ref[...] = jnp.cos(angle)
    sin_ref[...] = jnp.where(lane < half, -1.0, 1.0) * jnp.sin(angle)


def attend_body(home_rows, which, n_pieces, cos_ref, sin_ref, len_ref, kc_ref, vc_ref, *rest):
    pieces, done, (out, q_scr, new_scr, o_scr, total_scr) = rest[:n_pieces], rest[n_pieces:-5], rest[-5:]
    local_rows, head_dim = cos_ref.shape
    steps = local_rows // home_rows
    cached = kc_ref.shape[2]
    kv_heads = len(which)
    heads = q_scr.shape[0] // (kv_heads * local_rows)
    width_q = heads * head_dim
    scale = 1.0 / math.sqrt(head_dim)
    cos, sin = cos_ref[...], sin_ref[...]

    def rope(v):
        return v * cos + pltpu.roll(v, head_dim // 2, 1) * sin

    def projected(h, begin):
        return sum(piece[h, :local_rows, begin : begin + head_dim].astype(F32) for piece in pieces)

    row, col = iota((local_rows, local_rows), 0), iota((local_rows, local_rows), 1)
    live = (row % home_rows == col % home_rows) & (col // home_rows <= row // home_rows)
    per_row = heads * steps
    spot_ids = iota((per_row, cached), 1).astype(F32)
    every = [(h, b) for h in range(kv_heads) for b in range(home_rows)]
    mine = {
        (h, b): pl.ds(h * heads * local_rows + b, per_row, stride=home_rows) for h, b in every
    }
    new_weights, values_new = {}, {}
    for h in range(kv_heads):
        key_new = rope(projected(h, width_q)).astype(BF16)
        values_new[h] = projected(h, width_q + head_dim).astype(BF16)
        for n in range(heads):
            query = rope(projected(h, n * head_dim)).astype(BF16)
            here = slice((h * heads + n) * local_rows, (h * heads + n + 1) * local_rows)
            q_scr[here, :] = query.astype(F32)
            weight = jnp.where(live, jnp.exp(nt(query, key_new) * scale), 0.0)
            new_weights[h, n] = weight
            new_scr[here, :] = jnp.broadcast_to(jnp.sum(weight, 1, keepdims=True), (local_rows, head_dim))
    for h in range(kv_heads):
        scores = [nt(q_scr[mine[h, b], :].astype(BF16), kc_ref[b, which[h]]) for b in range(home_rows)]
        probs = []
        for b in range(home_rows):
            weight = jnp.where(spot_ids < len_ref[b : b + 1, :], jnp.exp(scores[b] * scale), 0.0)
            total = jnp.sum(weight, 1, keepdims=True) + new_scr[mine[h, b], :][:, :1]
            total_scr[mine[h, b], :] = jnp.broadcast_to(total, (per_row, head_dim))
            probs.append((weight / total).astype(BF16))
        for b in range(home_rows):
            o_scr[mine[h, b], :] = nn(probs[b], vc_ref[b, which[h]])
    for h in range(kv_heads):
        for n in range(heads):
            at = h * heads + n
            here = slice(at * local_rows, (at + 1) * local_rows)
            prob = (new_weights[h, n] / total_scr[here, :local_rows]).astype(BF16)
            out[:, at * head_dim : (at + 1) * head_dim] = (
                o_scr[here, :] + nn(prob, values_new[h])
            ).astype(BF16)
    for piece in done:
        out[:, kv_heads * width_q :] = piece[...]


def on_device(
    hidden,
    query_weight,
    key_weight,
    value_weight,
    key_cache_rows,
    value_cache_rows,
    adapter_down_weight,
    adapter_up_query,
    adapter_up_value,
    request_adapter,
    row_request,
    lengths,
):
    homes = lax.axis_size("pool")
    features = lax.axis_size(FEATURE_AXES)
    home_rows, kv_here, cached, head_dim = key_cache_rows.shape
    rows, steps, slice_width = hidden.shape
    resident = adapter_down_weight.shape[0]
    rank = adapter_up_query.shape[1]
    q_cols = query_weight.shape[1] // kv_here
    cap = max(2, 2 * home_rows // homes)
    places = homes * cap
    fold = homes // features
    local_rows = steps * home_rows
    width = q_cols + 2 * head_dim
    shape = jax.ShapeDtypeStruct

    if homes == len(CARRIER) and features == len(CARRIER):
        targets = [[CARRIER[q].index(g) for g in range(features)] for q in range(homes)]
        perms = [[(q * features + g, targets[q][g] * features + q) for q in range(homes) for g in range(features)]]

        def owners():
            pool_here, feature_here = lax.axis_index("pool"), lax.axis_index(FEATURE_AXES)
            at = pool_here * features + feature_here
            owner = jnp.int32(0)
            for q in range(homes):
                for g in range(features):
                    owner = jnp.where(at == q * features + g, targets[q][g], owner)
            return [owner]

    else:
        perms = [
            [
                (q * features + g, (g * fold + (i + q) % fold) * features + q // fold)
                for q in range(homes)
                for g in range(features)
            ]
            for i in range(fold)
        ]

        def owners():
            pool_here, feature_here = lax.axis_index("pool"), lax.axis_index(FEATURE_AXES)
            return [feature_here * fold + lax.rem(pool_here + i, fold) for i in range(fold)]

    rr, ra, ln = row_request.reshape(1, rows), request_adapter.reshape(1, rows), lengths.reshape(1, rows)
    by_step = hidden.transpose(1, 0, 2)
    x = by_step.reshape(steps * rows, slice_width)
    halved = kv_here // 2 if homes == 4 else 0

    *selected, facts = call(
        functools.partial(select_body, home_rows, cap, resident, owners),
        [shape((steps * places, slice_width), BF16)] * fold + [shape((8, rows), F32)],
        (rr, ra, ln, by_step),
        in_specs=[HBM] * 4,
        limit=60,
        scratch=[pltpu.VMEM((1, rows), jnp.int32)] * 3
        + [pltpu.VMEM(by_step.shape, BF16), pltpu.SemaphoreType.DMA((4,))],
        flops=2 * steps * places * rows * slice_width,
        bytes_=2 * steps * (rows + places) * slice_width,
    )
    sent = [lax.ppermute(s, ("pool", *FEATURE_AXES), perm) for s, perm in zip(selected, perms)]

    def swap(value, d):
        return lax.ppermute(value, "pool", [(i, i ^ d) for i in range(homes)])

    weights = (x, query_weight, key_weight, value_weight)

    def weight_specs(first):
        return [
            pl.BlockSpec(x.shape, lambda i: (0, 0)),
            pl.BlockSpec((slice_width, q_cols), lambda i: (0, first + i)),
            pl.BlockSpec((slice_width, head_dim), lambda i: (0, first + i)),
            pl.BlockSpec((slice_width, head_dim), lambda i: (0, first + i)),
        ]

    partials, facts = call(
        project_body,
        [shape((kv_here, steps * rows, width), BF16), shape(facts.shape, F32)],
        (*weights, facts),
        in_specs=weight_specs(0) + [pl.BlockSpec(facts.shape, lambda i: (0, 0))],
        out_specs=[
            pl.BlockSpec((1, steps * rows, width), lambda i: (i, 0, 0)),
            pl.BlockSpec(facts.shape, lambda i: (0, 0)),
        ],
        grid=(kv_here,),
        limit=50,
        flops=2 * steps * rows * slice_width * width * kv_here,
        bytes_=2 * slice_width * width * kv_here,
    )
    share = call(
        functools.partial(shrink_body, home_rows, cap, resident, fold),
        shape((steps * places, 2 * rank), BF16),
        (facts, adapter_down_weight, *sent),
        flops=4 * steps * places * rank * slice_width * fold * resident,
        bytes_=4 * resident * rank * slice_width * fold,
    )
    shares = [share] + [
        lax.ppermute(share, FEATURE_AXES, [(i, i ^ d) for i in range(features)]) for d in range(1, features)
    ]
    cos, sin, length = call(
        functools.partial(home_body, home_rows),
        [shape((local_rows, head_dim), F32)] * 2 + [shape((home_rows, cached), F32)],
        (facts,),
        flops=10**7,
        bytes_=10**5,
    )
    pair = shape((halved, 2 * local_rows, width), BF16)
    message = shape((kv_here - halved, local_rows, width), BF16)

    direct = tuple(range(halved, kv_here))
    pair = shape((halved, 2 * local_rows, width), BF16)
    grown = call(
        functools.partial(expand_body, home_rows, homes, halved),
        [pair] * (2 if halved else 0) + [shape((len(direct), local_rows, width), BF16)] * homes,
        (facts, adapter_up_query, adapter_up_value, *shares, partials),
        scratch=[pltpu.VMEM((steps * rows, width), F32)],
        flops=2 * steps * places * rank * resident * q_cols * kv_here,
        bytes_=2 * resident * rank * q_cols * kv_here,
    )
    messages = list(grown[-homes:])
    for d in reversed(range(2, homes)):
        messages[d] = swap(messages[d], d)
    sums = ()
    if halved:
        near, far = grown[:2]
        got = swap(far, 1)
        passed, messages[1] = call(
            add_body,
            [shape((halved, local_rows, width), BF16), shape(messages[1].shape, BF16)],
            (near, got, messages[1]),
            flops=halved * local_rows * width,
            bytes_=10 * halved * local_rows * width,
        )
        sums = (near, got, swap(passed, 2))
    messages[1] = swap(messages[1], 1)

    def attend(heads, pieces, done):
        return call(
            functools.partial(attend_body, home_rows, heads, len(pieces)),
            shape((local_rows, q_cols * (len(heads) + (len(direct) if done else 0))), BF16),
            (cos, sin, length, key_cache_rows, value_cache_rows, *pieces, *done),
            scratch=[pltpu.VMEM((len(heads) * q_cols // head_dim * local_rows, head_dim), F32)] * 4,
            flops=4 * local_rows * q_cols * len(heads) * cached,
            bytes_=4 * home_rows * cached * head_dim * len(heads),
        )

    out = attend(direct, messages, ())
    if halved:
        out = attend(tuple(range(halved)), sums, (out,))
    return out.reshape(steps, home_rows, q_cols * kv_here).transpose(1, 0, 2)


def solution(mesh):
    return jax.shard_map(
        on_device,
        mesh=mesh,
        in_specs=(
            P("groups", None, "pool"),
            P("pool", ("tp", "sub")),
            P("pool", ("tp", "sub")),
            P("pool", ("tp", "sub")),
            P(("groups", "pool"), ("tp", "sub"), None, None),
            P(("groups", "pool"), ("tp", "sub"), None, None),
            P(("groups", "pool"), None, ("tp", "sub")),
            P(("groups", "pool"), None, ("tp", "sub")),
            P(("groups", "pool"), None, ("tp", "sub")),
            P("groups"),
            P("groups"),
            P("groups"),
        ),
        out_specs=P(("groups", "pool"), None, ("tp", "sub")),
        check_vma=False,
    )
```
